128 devices in a mesh: win: 32 (over x, z, core), rep: 4 (over y).
Axes of the slice: x: 4, y: 4, z: 4, core: 2. Of those that a mesh axis runs over, the one named last changes fastest.
Arguments:
- events: bfloat16 [32, 4, 256, 768], P('win', 'rep'), may hold values from -8 to 8
- send_counts: int32 [32, 4, 32], P('win', 'rep'), may hold values from 0 to 16, as said below
- patient_ids: int32 [32, 4, 256], P('win', 'rep'), may hold values from 0 to 15
- codes: int32 [32, 4, 256], P('win', 'rep'), may hold values from 0 to 4095
- event_piece: int32 [32, 4, 256], P('win', 'rep'), may hold values from 0 to 7
- censor_piece: int32 [32, 4, 256], P('win', 'rep'), may hold values from 0 to 7
- norm_gain: float32 [768], replicated, may hold values from 0.5 to 1.5
- w_qkv: bfloat16 [768, 2304], replicated, may hold values from -1 to 1
- w_out: bfloat16 [768, 768], replicated, may hold values from -0.21875 to 0.21875
- w_piece: bfloat16 [768, 1024], replicated, may hold values from -0.21875 to 0.21875
- code_table: bfloat16 [4096, 128], replicated, may hold values from -0.5 to 0.5
Outputs:
- grad_events: bfloat16 [32, 4, 256, 768], P('win', 'rep')
- grad_gain: float32 [768], P(('win', 'rep'))
- grad_qkv: float32 [768, 2304], P(('win', 'rep'))
- grad_out: float32 [768, 768], P(('win', 'rep'))
- grad_piece: float32 [768, 1024], P(('win', 'rep'))
- grad_table: float32 [4096, 128], P(('win', 'rep'))
The draws below stay inside these ranges and needn't reach their ends.
Inputs may be any that keep to these rules, and one draw needn't show every extreme that they name: `send_counts`: every device's counts sum to 256. In every replica group one owner receives 16 events from every device, 512 in all; no owner receives more than 512.
All inputs are finite; a program needn't handle non-finite values.
Results may differ from the reference program's by a relative error of at most 0.018.
The reference program's roundings to bfloat16 on the way count: a program that leaves them out, or rounds other values in their place, can miss the bound.
Values may be sent and summed in bfloat16 or wider, within the bound.
A program may use at most 128 MiB of HBM per device.

```python
import functools
import math
import jax
import jax.numpy as jnp
import numpy as np
from jax import lax

D = 768
HEADS = 12
PIECES = 8
CODES = 4096
R = 128
CAP = 512
PATIENTS = 16
EV_DEV = 256
N_WIN = 32
N_REP = 4


def draw_send_counts(key, part):
    key = jax.random.fold_in(key, 11)
    slot_len = CAP // N_WIN
    half_slot = slot_len // 2
    hot_key, row_key = jax.random.split(key)
    hot_owner = jax.random.randint(hot_key, (N_REP,), 0, N_WIN)
    row_keys = jax.random.split(row_key, N_WIN * N_REP)
    hot_grid = jnp.broadcast_to(hot_owner[None, :], (N_WIN, N_REP)).reshape(-1)

    def one_source(source_key, hot_index):
        perm_key, size_key = jax.random.split(source_key)
        order_perm = jax.random.permutation(perm_key, N_WIN - 1)
        amount = jax.random.randint(size_key, ((N_WIN - 2) // 2,), 0, half_slot + 1)
        paired = jnp.stack([amount, -amount], 1).reshape(-1).astype(jnp.int32)
        sequence = jnp.concatenate([jnp.full((1,), -half_slot, jnp.int32), paired])
        relative = jnp.zeros((N_WIN - 1,), jnp.int32).at[order_perm].set(sequence)
        row_counts = jnp.concatenate([jnp.full((1,), half_slot, jnp.int32), relative]) + half_slot
        return jnp.roll(row_counts, hot_index)
    return jax.vmap(one_source)(row_keys, hot_grid).reshape(N_WIN, N_REP, N_WIN).astype(jnp.int32)


def draw_events(key, part):
    key = jax.random.fold_in(key, 5)
    full_shape = (N_WIN, N_REP, EV_DEV, D)
    result = jax.random.normal(key, full_shape)
    return jnp.clip(result, -8.0, 8.0).astype(jnp.bfloat16)


def draw_w_qkv(key, part):
    key = jax.random.fold_in(key, 6)
    result = jax.random.normal(key, (D, 3 * D)) / math.sqrt(D)
    return jnp.clip(result, -1.0, 1.0).astype(jnp.bfloat16)


def plant(entries, key, least, high):
    place = [jax.random.randint(jax.random.fold_in(key, axis), (), 0, length) for axis, length in enumerate(entries.shape)]
    widest = entries.shape.index(max(entries.shape))
    next_to = place[:widest] + [(place[widest] + 1) % entries.shape[widest]] + place[widest + 1:]
    return entries.at[tuple(place)].set(least).at[tuple(next_to)].set(high)


def cumulative_ranks(number_of, slope):
    portions = [(1 << 20) // math.isqrt(rank ** slope) + 1 for rank in range(1, number_of + 1)]
    spread = 1 + sum(portions) // (1 << 30)
    return np.cumsum(np.array([max(1, weight // spread) for weight in portions]))


def ranked_ids(rng, extent, count, slope):
    table = cumulative_ranks(count, slope)
    ticket = jax.random.randint(jax.random.fold_in(rng, 1), extent, 0, int(table[count - 1]))
    grade = jnp.searchsorted(jnp.asarray(table, jnp.int32), ticket, side="right")
    return jax.random.permutation(jax.random.fold_in(rng, 2), count)[grade].astype(jnp.int32)


def normal_values(rng, dims, spread, most, kind=jnp.bfloat16):
    return jnp.clip(spread * jax.random.normal(rng, dims, jnp.float32), -most, most).astype(kind)


def setup_inputs(seed: int = 0) -> dict:
    keys = jax.random.split(jax.random.key(seed), 12)
    events = draw_events(jax.random.fold_in(keys[11], 71), 0)
    send_counts = draw_send_counts(jax.random.fold_in(keys[11], 71), 0)
    patient_ids = plant(jax.random.randint(keys[2], (N_WIN, N_REP, EV_DEV), 0, PATIENTS), jax.random.fold_in(keys[2], 1), 0, PATIENTS - 1).astype(jnp.int32)
    codes = plant(ranked_ids(keys[3], (N_WIN, N_REP, EV_DEV), CODES, 2), jax.random.fold_in(keys[3], 3), 0, CODES - 1).astype(jnp.int32)
    event_piece = plant(jax.random.randint(keys[4], (N_WIN, N_REP, EV_DEV), 0, PIECES), jax.random.fold_in(keys[4], 1), 0, PIECES - 1).astype(jnp.int32)
    censor_piece = plant(jax.random.randint(keys[5], (N_WIN, N_REP, EV_DEV), 0, PIECES), jax.random.fold_in(keys[5], 1), 0, PIECES - 1).astype(jnp.int32)
    norm_gain = jnp.clip(1.0 + 0.1 * jax.random.normal(keys[6], (D,), jnp.float32), 0.5, 1.5)
    w_qkv = draw_w_qkv(jax.random.fold_in(keys[11], 71), 0)
    w_out = normal_values(keys[8], (D, D), D ** -0.5, 0.21875)
    w_piece = normal_values(keys[9], (D, PIECES * R), D ** -0.5, 0.21875)
    code_table = normal_values(keys[10], (CODES, R), R ** -0.5, 0.5)
    return {"events": events, "send_counts": send_counts, "patient_ids": patient_ids, "codes": codes, "event_piece": event_piece, "censor_piece": censor_piece, "norm_gain": norm_gain, "w_qkv": w_qkv, "w_out": w_out, "w_piece": w_piece, "code_table": code_table}


EPSILON = 1e-05

def pack_rows(source, labels, counts, slot_len):
    total_rows = source.shape[0]
    starts = jnp.cumsum(counts, dtype=jnp.int32) - counts
    offset = jnp.arange(slot_len, dtype=jnp.int32)
    take_index = jnp.clip(starts[:, None] + offset[None, :], 0, total_rows - 1)
    filled = offset[None, :] < counts[:, None]
    packed = jnp.where(filled[:, :, None], source[take_index], jnp.zeros((), source.dtype))
    packed_labels = jnp.where(filled[:, :, None], labels[take_index], 0).astype(jnp.int32)
    return (packed, packed_labels)

def unpack_rows(returned, counts, total_rows):
    slot_len = returned.shape[1]
    sources = counts.shape[0]
    ends_at = jnp.cumsum(counts, dtype=jnp.int32)
    starts = ends_at - counts
    position = jnp.arange(total_rows, dtype=jnp.int32)
    owner_of = jnp.minimum(lax.optimization_barrier(jnp.sum((ends_at[None, :] <= position[:, None]).astype(jnp.int32), 1, dtype=jnp.int32)), sources - 1)
    chosen = owner_of[:, None] == jnp.arange(sources, dtype=jnp.int32)[None, :]
    first_slot = lax.optimization_barrier(jnp.sum(jnp.where(chosen, starts[None, :], 0), 1, dtype=jnp.int32))
    flat_index = (owner_of * slot_len + position - first_slot).astype(jnp.int32)
    return returned.reshape(-1, returned.shape[2])[flat_index]

def compact(received, received_labels, counts, block_len):
    sources, slot_len, row_width = received.shape
    ends_at = jnp.cumsum(counts, dtype=jnp.int32)
    starts = ends_at - counts
    position = jnp.arange(block_len, dtype=jnp.int32)
    source_of = jnp.minimum(lax.optimization_barrier(jnp.sum((ends_at[None, :] <= position[:, None]).astype(jnp.int32), 1, dtype=jnp.int32)), sources - 1)
    chosen = source_of[:, None] == jnp.arange(sources, dtype=jnp.int32)[None, :]
    first_slot = lax.optimization_barrier(jnp.sum(jnp.where(chosen, starts[None, :], 0), 1, dtype=jnp.int32))
    is_valid = position < ends_at[-1]
    flat_index = jnp.clip(source_of * slot_len + position - first_slot, 0, sources * slot_len - 1).astype(jnp.int32)
    event_block = jnp.where(is_valid[:, None], received.reshape(-1, row_width)[flat_index], jnp.zeros((), received.dtype))
    labels = received_labels.reshape(-1, received_labels.shape[2])[flat_index]
    return (event_block, labels, is_valid, starts)

def uncompact(grad_block, starts, counts, slot_len):
    block_len = grad_block.shape[0]
    offset = jnp.arange(slot_len, dtype=jnp.int32)
    take_index = jnp.clip(starts[:, None] + offset[None, :], 0, block_len - 1).astype(jnp.int32)
    filled = offset[None, :] < counts[:, None]
    return jnp.where(filled[:, :, None], grad_block[take_index], jnp.zeros((), grad_block.dtype))

def softmax_rows(query_head, key_head, allowed, score_scale):
    scores = jnp.dot(query_head, key_head.T, preferred_element_type=jnp.float32) * score_scale
    masked = jnp.where(allowed, scores, -1e+30)
    row_max = lax.optimization_barrier(jnp.max(masked, -1, keepdims=True))
    weights = jnp.where(allowed, jnp.exp(masked - row_max), 0.0)
    return weights / lax.optimization_barrier(jnp.sum(weights, -1, keepdims=True))

def layer_forward(event_block, patient, norm_gain, w_qkv, w_out):
    block_len, row_width = event_block.shape
    head_dim = row_width // HEADS
    score_scale = 1.0 / math.sqrt(head_dim)
    x_float = event_block.astype(jnp.float32)
    mean_sq = lax.optimization_barrier(jnp.mean(x_float * x_float, -1, keepdims=True))
    inv_rms = lax.rsqrt(mean_sq + EPSILON)
    x_hat = x_float * inv_rms
    normed = (x_hat * norm_gain).astype(jnp.bfloat16)
    qkv_all = jnp.dot(normed, w_qkv, preferred_element_type=jnp.float32).astype(jnp.bfloat16)
    per_head = qkv_all.reshape(block_len, 3, HEADS, head_dim).transpose(1, 2, 0, 3)
    position = jnp.arange(block_len, dtype=jnp.int32)
    allowed = (patient[:, None] == patient[None, :]) & (position[None, :] <= position[:, None]) | (position[:, None] == position[None, :])

    def attend(head_inputs):
        query_head, key_head, values = head_inputs
        prob_rows = softmax_rows(query_head, key_head, allowed, score_scale).astype(jnp.bfloat16)
        return jnp.dot(prob_rows, values, preferred_element_type=jnp.float32).astype(jnp.bfloat16)
    context_heads = lax.map(attend, (per_head[0], per_head[1], per_head[2]))
    context = context_heads.transpose(1, 0, 2).reshape(block_len, row_width)
    attn_out = jnp.dot(context, w_out, preferred_element_type=jnp.float32)
    hidden = (x_float + attn_out).astype(jnp.bfloat16)
    return (hidden, (x_hat, inv_rms, normed, per_head, context, allowed))

def layer_backward(grad_hidden, saved_state, norm_gain, w_qkv, w_out):
    x_hat, inv_rms, normed, per_head, context, allowed = saved_state
    block_len, row_width = grad_hidden.shape
    head_dim = row_width // HEADS
    score_scale = 1.0 / math.sqrt(head_dim)
    grad_wout = jnp.dot(context.T, grad_hidden, preferred_element_type=jnp.float32)
    grad_context = jnp.dot(grad_hidden, w_out.T, preferred_element_type=jnp.float32).astype(jnp.bfloat16)
    grad_heads = grad_context.reshape(block_len, HEADS, head_dim).transpose(1, 0, 2)

    def backward_head(head_inputs):
        query_head, key_head, values, upstream = head_inputs
        prob_rows = softmax_rows(query_head, key_head, allowed, score_scale)
        prob_low = prob_rows.astype(jnp.bfloat16)
        grad_probs = jnp.dot(upstream, values.T, preferred_element_type=jnp.float32)
        grad_values = jnp.dot(prob_low.T, upstream, preferred_element_type=jnp.float32)
        inner_sum = lax.optimization_barrier(jnp.sum(grad_probs * prob_rows, -1, keepdims=True))
        grad_scores = (prob_rows * (grad_probs - inner_sum) * score_scale).astype(jnp.bfloat16)
        grad_query = jnp.dot(grad_scores, key_head, preferred_element_type=jnp.float32)
        grad_keys = jnp.dot(grad_scores.T, query_head, preferred_element_type=jnp.float32)
        return jnp.stack([grad_query, grad_keys, grad_values])
    stacked = lax.map(backward_head, (per_head[0], per_head[1], per_head[2], grad_heads))
    grad_qkv_rows = stacked.transpose(2, 1, 0, 3).reshape(block_len, 3 * row_width).astype(jnp.bfloat16)
    grad_wqkv = jnp.dot(normed.T, grad_qkv_rows, preferred_element_type=jnp.float32)
    grad_normed = jnp.dot(grad_qkv_rows, w_qkv.T, preferred_element_type=jnp.float32)
    grad_gain = lax.optimization_barrier(jnp.sum(grad_normed * x_hat, 0))
    grad_hat = grad_normed * norm_gain
    grad_float = inv_rms * (grad_hat - x_hat * lax.optimization_barrier(jnp.mean(grad_hat * x_hat, -1, keepdims=True)))
    grad_block = (grad_float + grad_hidden.astype(jnp.float32)).astype(jnp.bfloat16)
    return (grad_block, grad_gain, grad_wqkv, grad_wout)

def hazard_rows(piece_reps, is_valid, target_code, event_ids, end_ids, code_table):
    row_count = piece_reps.shape[0]
    codes_total, rep_width = code_table.shape
    pieces_total = piece_reps.shape[1] // rep_width
    piece_stack = piece_reps.reshape(row_count, pieces_total, rep_width).transpose(1, 0, 2)
    code_ids = jnp.arange(codes_total, dtype=jnp.int32)
    is_code = target_code[:, None] == code_ids[None, :]
    last_piece = jnp.where(is_code, event_ids[:, None], end_ids[:, None])
    log_codes = math.log(codes_total)

    def one_piece(running, piece_inputs):
        reps_now, piece_index = piece_inputs
        logits = jnp.dot(reps_now, code_table.T, preferred_element_type=jnp.float32) - log_codes
        live_mask = (piece_index <= last_piece) & is_valid[:, None]
        target = is_code & (event_ids[:, None] == piece_index) & is_valid[:, None]
        grad_logits = (jnp.where(live_mask, jnp.exp(logits), 0.0) - target.astype(jnp.float32)).astype(jnp.bfloat16)
        running = running + jnp.dot(grad_logits.T, reps_now, preferred_element_type=jnp.float32)
        return (running, jnp.dot(grad_logits, code_table, preferred_element_type=jnp.float32))
    zero_table = jnp.zeros((codes_total, rep_width), jnp.float32)
    grad_table, grad_stack = lax.scan(one_piece, zero_table, (piece_stack, jnp.arange(pieces_total, dtype=jnp.int32)))
    grad_reps = grad_stack.transpose(1, 0, 2).reshape(row_count, pieces_total * rep_width)
    return (grad_reps, grad_table)

def owner_step(received, received_labels, counts_in, block_len, split_rows, norm_gain, w_qkv, w_out, w_piece, code_table):
    event_block, labels, is_valid, starts = compact(received, received_labels, counts_in, block_len)
    patient = jnp.where(is_valid, labels[:, 0], -1)
    hidden, saved_state = layer_forward(event_block, patient, norm_gain, w_qkv, w_out)
    piece_reps = jnp.dot(hidden, w_piece, preferred_element_type=jnp.float32).astype(jnp.bfloat16)
    grad_reps, grad_table = hazard_rows(piece_reps, is_valid, labels[:, 1], labels[:, 2], labels[:, 3], code_table)
    grad_low = grad_reps.astype(jnp.bfloat16)
    grad_wpiece = jnp.dot(hidden.T, grad_low, preferred_element_type=jnp.float32)
    grad_hidden = jnp.dot(grad_low, w_piece.T, preferred_element_type=jnp.float32).astype(jnp.bfloat16)
    grad_block, grad_gain, grad_wqkv, grad_wout = layer_backward(grad_hidden, saved_state, norm_gain, w_qkv, w_out)
    grad_slots = uncompact(grad_block, starts, counts_in, received.shape[1])
    return (grad_slots, (grad_gain, grad_wqkv, grad_wout, grad_wpiece, grad_table))

def reference(events, send_counts, patient_ids, codes, event_piece, censor_piece, norm_gain, w_qkv, w_out, w_piece, code_table):
    win_count, rep_count, total_rows, row_width = events.shape
    block_len = 2 * total_rows
    slot_len = block_len // win_count
    end_piece = jnp.maximum(event_piece, censor_piece)
    labels = jnp.stack([patient_ids, codes, event_piece, end_piece], -1).astype(jnp.int32)
    packer = functools.partial(pack_rows, slot_len=slot_len)
    unpacker = functools.partial(unpack_rows, total_rows=total_rows)
    totals = (jnp.zeros(norm_gain.shape, jnp.float32), jnp.zeros(w_qkv.shape, jnp.float32), jnp.zeros(w_out.shape, jnp.float32), jnp.zeros(w_piece.shape, jnp.float32), jnp.zeros(code_table.shape, jnp.float32))
    replica_rows = []
    for replica in range(rep_count):
        packed, packed_labels = jax.vmap(packer)(events[:, replica], labels[:, replica], send_counts[:, replica])

        def owner_turn(running, owner_index):
            received = packed[:, owner_index]
            received_labels = packed_labels[:, owner_index]
            counts_in = send_counts[:, replica, owner_index]
            grad_slots, weight_grads = owner_step(received, received_labels, counts_in, block_len, False, norm_gain, w_qkv, w_out, w_piece, code_table)
            running = tuple((left + right for left, right in zip(running, weight_grads)))
            return (running, grad_slots)
        totals, slots_all = lax.scan(owner_turn, totals, jnp.arange(win_count, dtype=jnp.int32))
        returned = slots_all.transpose(1, 0, 2, 3)
        replica_rows.append(jax.vmap(unpacker)(returned, send_counts[:, replica]))
    grad_events = jnp.stack(replica_rows, 1)
    factor = 1.0 / math.sqrt(total_rows * win_count * rep_count)
    return (grad_events, totals[0] * factor, totals[1] * factor, totals[2] * factor, totals[3] * factor, totals[4] * factor)
```

```python
import functools
import math

import jax
import jax.numpy as jnp
from jax import lax
from jax.experimental import pallas as pl
from jax.experimental.pallas import tpu as pltpu
from jax.sharding import PartitionSpec as P

HEADS = 12
EPSILON = 1e-05
MESH = pl.DeviceIdType.MESH

D = 768
PAIRS = 6
PIECES = 8
CODES = 4096
R = 128
ROWS = 512
EVENTS = 256
WIN = 32
SLOT = 16
LAB = 128
WIDE = D + LAB
BLOCK = 512

F32 = jnp.float32
BF16 = jnp.bfloat16

NT = (((1,), (1,)), ((), ()))
TN = (((0,), (0,)), ((), ()))


def mm(a, b):
    return jnp.dot(a, b, preferred_element_type=F32)


def mm_nt(a, b):
    return lax.dot_general(a, b, NT, preferred_element_type=F32)


def mm_tn(a, b):
    return lax.dot_general(a, b, TN, preferred_element_type=F32)


def exchange_rows(src_ref, dst_ref, send_sem, recv_sem, me):
    @pl.loop(1, WIN)
    def _(k):
        peer = lax.rem(me + k, WIN)
        pltpu.make_async_remote_copy(
            src_ref=src_ref.at[peer],
            dst_ref=dst_ref.at[me],
            send_sem=send_sem.at[k],
            recv_sem=recv_sem.at[k],
            device_id={"win": peer},
            device_id_type=MESH,
        ).start()


def wait_rows(src_ref, dst_ref, send_sem, recv_sem, me):
    @pl.loop(1, WIN)
    def _(k):
        sender = lax.rem(me + WIN - k, WIN)
        pltpu.make_async_remote_copy(
            src_ref=src_ref.at[me],
            dst_ref=dst_ref.at[sender],
            send_sem=send_sem.at[k],
            recv_sem=recv_sem.at[k],
            device_id={"win": sender},
            device_id_type=MESH,
        ).wait()


def dispatch_kernel(ev_ref, lab_ref, cnt_ref, out_ref, hot_ref, packed, landed, send_sem, recv_sem):
    me = lax.axis_index("win")
    barrier = pltpu.get_barrier_semaphore()

    @pl.loop(1, WIN)
    def _(k):
        pl.semaphore_signal(
            barrier, inc=1, device_id={"win": lax.rem(me + k, WIN)}, device_id_type=MESH
        )

    counts = cnt_ref[...].astype(F32)
    row = lax.broadcasted_iota(jnp.int32, (ROWS, WIN), 0)
    owner = lax.broadcasted_iota(jnp.int32, (ROWS, WIN), 1)
    row_owner = row // SLOT
    mine = jnp.sum(jnp.where(owner == row_owner, counts, 0.0), 1, keepdims=True)
    start = jnp.sum(jnp.where(owner < row_owner, counts, 0.0), 1, keepdims=True)
    offset = (lax.broadcasted_iota(jnp.int32, (ROWS, 1), 0) % SLOT).astype(F32)
    place = lax.broadcasted_iota(jnp.int32, (ROWS, EVENTS), 1).astype(F32)
    wanted = jnp.where(offset < mine, start + offset, -1.0)
    hot = jnp.where(place == wanted, 1.0, 0.0).astype(BF16)
    hot_ref[...] = hot
    packed[:, :, :D] = mm(hot, ev_ref[...]).astype(BF16).reshape(WIN, SLOT, D)

    lab = lab_ref[...]
    high = lab[1:2] // 64
    rows = [lab[0:1], high, lab[1:2] - high * 64, lab[2:3], jnp.maximum(lab[2:3], lab[3:4])]
    rows.append(jnp.ones((1, EVENTS), jnp.int32))
    rows.append(jnp.zeros((2, EVENTS), jnp.int32))
    table = jnp.concatenate(rows, 0).astype(F32)
    table = jnp.concatenate([table, jnp.zeros((LAB - 8, EVENTS), F32)], 0).astype(BF16)
    packed[:, :, D:] = mm_nt(hot, table).astype(BF16).reshape(WIN, SLOT, LAB)

    pl.semaphore_wait(barrier, WIN - 1)
    exchange_rows(packed, landed, send_sem, recv_sem, me)
    landed[me] = packed[me]
    wait_rows(packed, landed, send_sem, recv_sem, me)
    out_ref[...] = landed[...]


def dispatch(events, labels, counts):
    return pl.pallas_call(
        dispatch_kernel,
        out_shape=(
            jax.ShapeDtypeStruct((WIN, SLOT, WIDE), BF16),
            jax.ShapeDtypeStruct((ROWS, EVENTS), BF16),
        ),
        in_specs=[pl.BlockSpec(memory_space=pltpu.VMEM)] * 3,
        out_specs=(pl.BlockSpec(memory_space=pltpu.VMEM),) * 2,
        scratch_shapes=[
            pltpu.VMEM((WIN, SLOT, WIDE), BF16),
            pltpu.VMEM((WIN, SLOT, WIDE), BF16),
            pltpu.SemaphoreType.DMA((WIN,)),
            pltpu.SemaphoreType.DMA((WIN,)),
        ],
        compiler_params=pltpu.CompilerParams(
            collective_id=1, has_side_effects=True, vmem_limit_bytes=32 * 1024 * 1024
        ),
        name="dispatch",
    )(events, labels, counts)


def stack_halves(res):
    tiles = res.reshape(WIN, 3, 8, 256)
    both = jnp.concatenate([tiles[..., :128], tiles[..., 128:]], 2)
    return both.reshape(WIN, 48, 128).astype(BF16)


def lanes(index):
    return pl.ds(pl.multiple_of(index * 128, 128), 128)


def owner_kernel(
    x_ref,
    gain_ref,
    wqkv_ref,
    wout_ref,
    wpiece_ref,
    table_ref,
    gb_ref,
    sq_ref,
    so_ref,
    sp_ref,
    st_ref,
    sg_ref,
    normed,
    normed_t,
    qkv,
    prob,
    ctx,
    hidden,
    reps,
    reps_t,
    greps,
    glow,
    ghid,
    gctx,
    dqkv,
    bias,
    labs,
    gtab_t,
    gnorm,
):
    gain = gain_ref[...]
    lab = x_ref[:, D:].astype(F32)
    valid = lab[:, 5:6] > 0.5
    patient = jnp.where(valid, lab[:, 0:1], -1.0)
    labs[0] = jnp.broadcast_to(lab[:, 1:2] * 64.0 + lab[:, 2:3], (ROWS, 128))
    labs[1] = jnp.broadcast_to(jnp.where(valid, lab[:, 3:4], -1.0), (ROWS, 128))
    labs[2] = jnp.broadcast_to(jnp.where(valid, lab[:, 4:5], -1.0), (ROWS, 128))

    lab_t = lab.T
    patient_row = jnp.where(lab_t[5:6] > 0.5, lab_t[0:1], -1.0)
    row = lax.broadcasted_iota(jnp.int32, (ROWS, ROWS), 0)
    col = lax.broadcasted_iota(jnp.int32, (ROWS, ROWS), 1)
    allowed = ((patient == patient_row) & (col <= row)) | (col == row)
    bias[...] = jnp.where(allowed, 0.0, -1e30)

    x = x_ref[:, :D].astype(F32)
    inv_rms = lax.rsqrt(jnp.mean(x * x, -1, keepdims=True) + EPSILON)
    normed[...] = (x * inv_rms * gain).astype(BF16)

    @pl.loop(0, 9)
    def _(j):
        cols = pl.ds(pl.multiple_of(j * 256, 256), 256)
        res = mm(normed[...], wqkv_ref[:, cols])
        scale = jnp.where(j < 3, 0.125, 1.0)
        res = (res * scale).astype(BF16)
        qkv[2 * j] = res[:, :128]
        qkv[2 * j + 1] = res[:, 128:]

    low_lanes = lax.broadcasted_iota(jnp.int32, (1, 128), 1) < 64

    def head_part(value, head):
        zero = jnp.zeros((), value.dtype)
        return jnp.where(low_lanes, value, zero) if head == 0 else jnp.where(low_lanes, zero, value)

    @pl.loop(0, PAIRS)
    def _(p):
        q = qkv[p]
        k = qkv[PAIRS + p]
        v = qkv[2 * PAIRS + p]
        for rb in range(2):
            rs = slice(rb * 256, rb * 256 + 256)
            n = (rb + 1) * 256
            parts = []
            for head in range(2):
                s = mm_nt(head_part(q[rs], head), k[:n]) + bias[rs, :n]
                w = jnp.exp(s - jnp.max(s, -1, keepdims=True))
                pr = (w * (1.0 / jnp.sum(w, -1, keepdims=True))).astype(BF16)
                prob[p, head, rs, :n] = pr
                parts.append(mm(pr, v[:n]))
            ctx[rs, lanes(p)] = jnp.where(low_lanes, parts[0], parts[1]).astype(BF16)

    @pl.loop(0, 3)
    def _(j):
        cols = pl.ds(pl.multiple_of(j * 256, 256), 256)
        res = mm(ctx[...], wout_ref[:, cols])
        hidden[:, cols] = (x_ref[:, cols].astype(F32) + res).astype(BF16)

    @pl.loop(0, 4)
    def _(j):
        cols = pl.ds(pl.multiple_of(j * 256, 256), 256)
        res = mm(hidden[...], wpiece_ref[:, cols])
        for i in range(2):
            part = res[:, i * 128 : i * 128 + 128]
            reps[2 * j + i] = part.astype(BF16)
            reps_t[2 * j + i] = part.T.astype(BF16)

    log_codes = math.log(CODES)
    times = BLOCK // 128

    def widen(tile):
        return jnp.concatenate([tile] * times, 1)

    greps[...] = jnp.zeros_like(greps)

    @pl.loop(0, CODES // BLOCK)
    def _(b):
        codes_at = pl.ds(pl.multiple_of(b * BLOCK, BLOCK), BLOCK)
        tab = table_ref[codes_at, :]
        ids = (b * BLOCK + lax.broadcasted_iota(jnp.int32, (1, BLOCK), 1)).astype(F32)
        gtab_t[:, codes_at] = jnp.zeros((R, BLOCK), F32)

        @pl.loop(0, PIECES)
        def _(p):
            piece = p.astype(F32)
            code, event, end = labs[0], labs[1], labs[2]
            at_row = jnp.where(end >= piece, -log_codes, -1e30)
            at_code = jnp.where(event >= piece, -log_codes, -1e30)
            target = jnp.where(event == piece, 1.0, 0.0)
            logits = mm_nt(reps[p], tab)
            is_code = widen(code) == ids
            e = jnp.exp(logits + jnp.where(is_code, widen(at_code), widen(at_row)))
            g = (e - jnp.where(is_code, widen(target), 0.0)).astype(BF16)
            greps[p] += mm(g, tab)
            gtab_t[:, codes_at] += mm(reps_t[p], g)

        st_ref[codes_at, :] = gtab_t[:, codes_at].T.astype(BF16)

    for p in range(PIECES):
        glow[:, p * 128 : p * 128 + 128] = greps[p].astype(BF16)

    hidden_t = hidden[...].T
    for j in range(4):
        rhs = jnp.concatenate(
            [glow[:, j * 128 : j * 128 + 128], glow[:, 512 + j * 128 : 512 + j * 128 + 128]], 1
        )
        sp_ref[:, :, j * 128 : j * 128 + 128] = stack_halves(mm(hidden_t, rhs))

    for j in range(3):
        cols = slice(j * 256, j * 256 + 256)
        ghid[:, cols] = mm_nt(glow[...], wpiece_ref[cols, :]).astype(BF16)

    ctx_t = ctx[...].T
    for j in range(3):
        rhs = jnp.concatenate(
            [ghid[:, j * 128 : j * 128 + 128], ghid[:, 384 + j * 128 : 384 + j * 128 + 128]], 1
        )
        so_ref[:, :, j * 128 : j * 128 + 128] = stack_halves(mm(ctx_t, rhs))

    for j in range(3):
        cols = slice(j * 256, j * 256 + 256)
        gctx[:, cols] = mm_nt(ghid[...], wout_ref[cols, :]).astype(BF16)

    @pl.loop(0, PAIRS)
    def _(p):
        q = qkv[p]
        k = qkv[PAIRS + p]
        v = qkv[2 * PAIRS + p]
        g = gctx[:, lanes(p)]
        dk = [None, None]
        dv = [None, None]
        for rb in range(2):
            rs = slice(rb * 256, rb * 256 + 256)
            n = (rb + 1) * 256
            dq = []
            for head in range(2):
                gh = head_part(g[rs], head)
                qh = head_part(q[rs], head)
                pr_low = prob[p, head, rs, :n]
                pr = pr_low.astype(F32)
                dp = mm_nt(gh, v[:n])
                inner = jnp.sum(dp * pr, -1, keepdims=True)
                ds = (pr * (dp - inner)).astype(BF16)
                dq.append(mm(ds, k[:n]))
                dv_now = mm_tn(pr_low, gh)
                dk_now = mm_tn(ds, qh)
                for half in range(rb + 1):
                    hs = slice(half * 256, half * 256 + 256)
                    dv[half] = dv_now[hs] if dv[half] is None else dv[half] + dv_now[hs]
                    dk[half] = dk_now[hs] if dk[half] is None else dk[half] + dk_now[hs]
            dqkv[rs, lanes(p)] = (jnp.where(low_lanes, dq[0], dq[1]) * 0.125).astype(BF16)
        for half in range(2):
            hs = slice(half * 256, half * 256 + 256)
            dqkv[hs, lanes(PAIRS + p)] = dk[half].astype(BF16)
            dqkv[hs, lanes(2 * PAIRS + p)] = dv[half].astype(BF16)

    normed_t[...] = normed[...].T

    @pl.loop(0, 9)
    def _(j):
        rhs = jnp.concatenate([dqkv[:, lanes(j)], dqkv[:, lanes(9 + j)]], 1)
        sq_ref[:, :, lanes(j)] = stack_halves(mm(normed_t[...], rhs))

    for j in range(3):
        cols = slice(j * 256, j * 256 + 256)
        gnorm[:, cols] = mm_nt(dqkv[...], wqkv_ref[cols, :])

    x = x_ref[:, :D].astype(F32)
    inv_rms = lax.rsqrt(jnp.mean(x * x, -1, keepdims=True) + EPSILON)
    x_hat = x * inv_rms
    gn = gnorm[...]
    ggain = jnp.sum(gn * x_hat, 0, keepdims=True)
    gh = gn * gain
    gx = inv_rms * (gh - x_hat * jnp.mean(gh * x_hat, -1, keepdims=True))
    gb = (gx + ghid[...].astype(F32)).astype(BF16)
    gb_ref[...] = gb.reshape(WIN, SLOT, D)

    feature = lax.broadcasted_iota(jnp.int32, (ROWS, D), 1)
    block = lax.broadcasted_iota(jnp.int32, (ROWS, D), 0) // SLOT
    spread = jnp.where(feature // 24 == block, ggain, 0.0).astype(BF16)
    pick = lax.broadcasted_iota(jnp.int32, (D, 128), 0) % 24
    pick = jnp.where(pick == lax.broadcasted_iota(jnp.int32, (D, 128), 1), 1.0, 0.0).astype(BF16)
    sg_ref[...] = mm(spread, pick).astype(BF16).reshape(WIN, SLOT, 128)


def owner_step(x, gain, w_qkv, w_out, w_piece, table):
    vmem = pl.BlockSpec(memory_space=pltpu.VMEM)
    return pl.pallas_call(
        owner_kernel,
        out_shape=(
            jax.ShapeDtypeStruct((WIN, SLOT, D), BF16),
            jax.ShapeDtypeStruct((WIN, 48, 1152), BF16),
            jax.ShapeDtypeStruct((WIN, 48, 384), BF16),
            jax.ShapeDtypeStruct((WIN, 48, 512), BF16),
            jax.ShapeDtypeStruct((CODES, R), BF16),
            jax.ShapeDtypeStruct((WIN, SLOT, 128), BF16),
        ),
        in_specs=[vmem] * 6,
        out_specs=(vmem,) * 6,
        scratch_shapes=[
            pltpu.VMEM((ROWS, D), BF16),
            pltpu.VMEM((D, ROWS), BF16),
            pltpu.VMEM((18, ROWS, 128), BF16),
            pltpu.VMEM((PAIRS, 2, ROWS, ROWS), BF16),
            pltpu.VMEM((ROWS, D), BF16),
            pltpu.VMEM((ROWS, D), BF16),
            pltpu.VMEM((PIECES, ROWS, R), BF16),
            pltpu.VMEM((PIECES, R, ROWS), BF16),
            pltpu.VMEM((PIECES, ROWS, R), F32),
            pltpu.VMEM((ROWS, PIECES * R), BF16),
            pltpu.VMEM((ROWS, D), BF16),
            pltpu.VMEM((ROWS, D), BF16),
            pltpu.VMEM((ROWS, 3 * D), BF16),
            pltpu.VMEM((ROWS, ROWS), F32),
            pltpu.VMEM((3, ROWS, 128), F32),
            pltpu.VMEM((R, CODES), F32),
            pltpu.VMEM((ROWS, D), F32),
        ],
        compiler_params=pltpu.CompilerParams(vmem_limit_bytes=56 * 1024 * 1024),
        cost_estimate=pl.CostEstimate(
            flops=26_000_000_000, bytes_accessed=16_000_000, transcendentals=20_000_000
        ),
        name="owner_step",
    )(x, gain, w_qkv, w_out, w_piece, table)


ITEMS = (
    ("t", 128, 128, "zx"),
    ("p", 48, 512, "xz"),
    ("o", 48, 384, "zx"),
    ("q0", 48, 640, "xz"),
    ("q1", 48, 512, "zx"),
    ("g", 16, 128, "xz"),
)
N_ITEMS = len(ITEMS)


def remote(src, dst, sems, index, where):
    return pltpu.make_async_remote_copy(
        src_ref=src,
        dst_ref=dst,
        send_sem=sems[0].at[index],
        recv_sem=sems[1].at[index],
        device_id=where,
        device_id_type=MESH,
    )


def reduce_kernel(
    gb_ref, sq_ref, so_ref, sp_ref, st_ref, sg_ref, hot_ref, rows_ref, gain_ref, qkv_ref, out_ref, piece_ref, tab_ref, *scratch
):
    landed, send_rows, recv_rows, send_sem, recv_sem = scratch[:5]
    bufs = [scratch[5 + 7 * i : 12 + 7 * i] for i in range(N_ITEMS)]
    sems = (send_sem, recv_sem)
    me = lax.axis_index("win")
    y = lax.axis_index("rep")
    core = lax.rem(me, 2)
    z = lax.rem(me // 2, 4)
    x = me // 8

    barrier = pltpu.get_barrier_semaphore()

    @pl.loop(1, WIN)
    def _(k):
        pl.semaphore_signal(
            barrier, inc=1, device_id={"win": lax.rem(me + k, WIN)}, device_id_type=MESH
        )

    @pl.loop(1, 4)
    def _(k):
        pl.semaphore_signal(
            barrier, inc=1, device_id={"rep": lax.rem(y + k, 4)}, device_id_type=MESH
        )

    pl.semaphore_wait(barrier, WIN - 1 + 3)

    sources = {
        "t": st_ref,
        "p": sp_ref,
        "o": so_ref,
        "q0": sq_ref.at[:, :, :, :, pl.ds(0, 640)],
        "q1": sq_ref.at[:, :, :, :, pl.ds(640, 512)],
        "g": sg_ref,
    }

    def at_xz(ref, order, first, second=None):
        if order == "xz":
            return ref.at[first] if second is None else ref.at[first, second]
        return ref.at[:, first] if second is None else ref.at[second, first]

    def win_of(order, step, k):
        if order[step] == "x":
            return lax.rem(x + k, 4) * 8 + z * 2 + core
        return x * 8 + lax.rem(z + k, 4) * 2 + core

    def place_of(order, step, k):
        return lax.rem((x if order[step] == "x" else z) + k, 4)

    def core_copy(i):
        name = ITEMS[i][0]
        return remote(
            sources[name].at[:, :, 1 - core], bufs[i][0], sems, (i, 0), {"win": me + 1 - 2 * core}
        )

    def ring_copy(i, step, k):
        order = ITEMS[i][3]
        if step == 0:
            src = at_xz(bufs[i][1], order, place_of(order, 0, k))
        else:
            src = bufs[i][3].at[place_of(order, 1, k)]
        return remote(
            src,
            bufs[i][2 + 2 * step].at[k - 1],
            sems,
            (i, 1 + 3 * step + k - 1),
            {"win": win_of(order, step, k)},
        )

    def last_copy(i, k):
        return remote(
            bufs[i][5].at[lax.rem(y + k, 4)],
            bufs[i][6].at[k - 1],
            sems,
            (i, 7 + k - 1),
            {"rep": lax.rem(y + k, 4)},
        )

    for i in range(N_ITEMS):
        core_copy(i).start()
    exchange_rows(gb_ref, landed, send_rows, recv_rows, me)
    landed[me] = gb_ref[me]

    for i in range(N_ITEMS):
        core_copy(i).wait()
        src, got, acc = sources[ITEMS[i][0]], bufs[i][0], bufs[i][1]
        for a in range(4):

            @pl.loop(0, 4)
            def _(b):
                acc[a, b] = (src[a, b, core].astype(F32) + got[a, b].astype(F32)).astype(BF16)

        for k in (2, 1, 3):
            ring_copy(i, 0, k).start()

    for i in range(N_ITEMS):
        order = ITEMS[i][3]
        for k in (2, 1, 3):
            ring_copy(i, 0, k).wait()
        got, acc = bufs[i][2], bufs[i][3]

        @pl.loop(0, 4)
        def _(b):
            total = at_xz(bufs[i][1], order, place_of(order, 0, 0), b)[...].astype(F32)
            for k in range(3):
                total += got[k, b].astype(F32)
            acc[b] = total.astype(BF16)

        for k in (2, 1, 3):
            ring_copy(i, 1, k).start()

    for i in range(N_ITEMS):
        name, rows, width, order = ITEMS[i]
        for k in (2, 1, 3):
            ring_copy(i, 1, k).wait()
        got = bufs[i][4]
        total = bufs[i][3][place_of(order, 1, 0)].astype(F32)
        for k in range(3):
            total += got[k].astype(F32)
        low = bufs[i][5]
        if name == "t":
            low[...] = total.astype(BF16).reshape(4, 32, 128)
        elif name == "g":
            for yy in range(4):
                low[yy] = total.astype(BF16)
        else:
            wide = scratch[-1]
            wide[:, 24:] = jnp.zeros((2, 8, 640), F32)
            for half in range(2):
                for t in range(3):
                    at = t * 16 + half * 8
                    wide[half, t * 8 : t * 8 + 8, :width] = total[at : at + 8]
            for yy in range(4):
                both = jnp.concatenate(
                    [wide[0, 6 * yy : 6 * yy + 8, :width], wide[1, 6 * yy : 6 * yy + 8, :width]], 0
                )
                low[yy] = both.astype(BF16)
        for k in (2, 1, 3):
            last_copy(i, k).start()

    factor = 1.0 / math.sqrt(EVENTS * WIN * 4)
    for i in range(N_ITEMS):
        name, rows, width, order = ITEMS[i]
        for k in (2, 1, 3):
            last_copy(i, k).wait()
        got = bufs[i][6]
        total = bufs[i][5][y].astype(F32)
        for k in range(3):
            total += got[k].astype(F32)
        total = total * factor
        if name == "t":
            tab_ref[...] = total
        elif name == "g":
            gain_ref[...] = total[:8]
        else:
            dst, base, half = {
                "p": (piece_ref, 0, 512),
                "o": (out_ref, 0, 384),
                "q0": (qkv_ref, 0, 1152),
                "q1": (qkv_ref, 640, 1152),
            }[name]
            dst[:, base : base + width] = total[:6]
            dst[:, half + base : half + base + width] = total[8:14]

    wait_rows(gb_ref, landed, send_rows, recv_rows, me)
    rows_ref[...] = mm_tn(hot_ref[...], landed[...].reshape(ROWS, D)).astype(BF16)


def reduce_all(gb, sq, so, sp, st, sg, hot):
    vmem = pl.BlockSpec(memory_space=pltpu.VMEM)
    scratch = [
        pltpu.VMEM((WIN, SLOT, D), BF16),
        pltpu.SemaphoreType.DMA((WIN,)),
        pltpu.SemaphoreType.DMA((WIN,)),
        pltpu.SemaphoreType.DMA((N_ITEMS, 10)),
        pltpu.SemaphoreType.DMA((N_ITEMS, 10)),
    ]
    for name, rows, width, order in ITEMS:
        last = {"t": 32, "g": 16}.get(name, 16)
        scratch += [
            pltpu.VMEM((4, 4, rows, width), BF16),
            pltpu.VMEM((4, 4, rows, width), BF16),
            pltpu.VMEM((3, 4, rows, width), BF16),
            pltpu.VMEM((4, rows, width), BF16),
            pltpu.VMEM((3, rows, width), BF16),
            pltpu.VMEM((4, last, width), BF16),
            pltpu.VMEM((3, last, width), BF16),
        ]
    scratch.append(pltpu.VMEM((2, 32, 640), F32))
    return pl.pallas_call(
        reduce_kernel,
        out_shape=(
            jax.ShapeDtypeStruct((EVENTS, D), BF16),
            jax.ShapeDtypeStruct((8, 128), F32),
            jax.ShapeDtypeStruct((6, 3 * D), F32),
            jax.ShapeDtypeStruct((6, D), F32),
            jax.ShapeDtypeStruct((6, PIECES * R), F32),
            jax.ShapeDtypeStruct((32, R), F32),
        ),
        in_specs=[vmem] * 7,
        out_specs=(vmem,) * 6,
        scratch_shapes=scratch,
        compiler_params=pltpu.CompilerParams(
            collective_id=2, has_side_effects=True, vmem_limit_bytes=56 * 1024 * 1024
        ),
        name="reduce_all",
    )(
        gb,
        sq.reshape(4, 4, 2, 48, 1152),
        so.reshape(4, 4, 2, 48, 384),
        sp.reshape(4, 4, 2, 48, 512),
        st.reshape(4, 4, 2, 128, 128),
        sg.reshape(4, 4, 2, 16, 128),
        hot,
    )


def body(
    events,
    send_counts,
    patient_ids,
    codes,
    event_piece,
    censor_piece,
    norm_gain,
    w_qkv,
    w_out,
    w_piece,
    code_table,
):
    labels = jnp.concatenate([patient_ids[0], codes[0], event_piece[0], censor_piece[0]], 0)
    received, hot = dispatch(events[0, 0], labels, send_counts[0])
    gb, sq, so, sp, st, sg = owner_step(
        received.reshape(ROWS, WIDE), norm_gain[None], w_qkv, w_out, w_piece, code_table
    )
    rows, gain, g_qkv, g_out, g_piece, g_table = reduce_all(gb, sq, so, sp, st, sg, hot)
    y = lax.axis_index("rep")
    g_gain = lax.dynamic_slice(gain[0], (6 * y,), (6,))
    return (rows[None, None], g_gain, g_qkv, g_out, g_piece, g_table)


def solution(mesh):
    split = P("win", "rep")
    return jax.shard_map(
        body,
        mesh=mesh,
        in_specs=(split,) * 6 + (P(),) * 5,
        out_specs=(split,) + (P(("win", "rep")),) * 5,
        check_vma=False,
    )
```

```python
import functools
import math

import jax
import jax.numpy as jnp
from jax import lax
from jax.experimental import pallas as pl
from jax.experimental.pallas import tpu as pltpu
from jax.sharding import PartitionSpec as P

HEADS = 12
EPSILON = 1e-05
MESH = pl.DeviceIdType.MESH

D = 768
PAIRS = 6
PIECES = 8
CODES = 4096
R = 128
ROWS = 512
EVENTS = 256
WIN = 32
SLOT = 16
LAB = 128
WIDE = D + LAB
BLOCK = 2048

F32 = jnp.float32
BF16 = jnp.bfloat16

NT = (((1,), (1,)), ((), ()))
TN = (((0,), (0,)), ((), ()))


def mm(a, b):
    return jnp.dot(a, b, preferred_element_type=F32)


def mm_nt(a, b):
    return lax.dot_general(a, b, NT, preferred_element_type=F32)


def mm_tn(a, b):
    return lax.dot_general(a, b, TN, preferred_element_type=F32)


def exchange_rows(src_ref, dst_ref, send_sem, recv_sem, me):
    @pl.loop(1, WIN)
    def _(k):
        peer = lax.rem(me + k, WIN)
        pltpu.make_async_remote_copy(
            src_ref=src_ref.at[peer],
            dst_ref=dst_ref.at[me],
            send_sem=send_sem.at[k],
            recv_sem=recv_sem.at[k],
            device_id={"win": peer},
            device_id_type=MESH,
        ).start()


def wait_rows(src_ref, dst_ref, send_sem, recv_sem, me):
    @pl.loop(1, WIN)
    def _(k):
        sender = lax.rem(me + WIN - k, WIN)
        pltpu.make_async_remote_copy(
            src_ref=src_ref.at[me],
            dst_ref=dst_ref.at[sender],
            send_sem=send_sem.at[k],
            recv_sem=recv_sem.at[k],
            device_id={"win": sender},
            device_id_type=MESH,
        ).wait()


def stack_halves(res):
    tiles = res.reshape(WIN, 3, 8, 256)
    both = jnp.concatenate([tiles[..., :128], tiles[..., 128:]], 2)
    return both.reshape(WIN, 48, 128).astype(BF16)


def lanes(index):
    return pl.ds(pl.multiple_of(index * 128, 128), 128)


ITEMS = (
    ("t", 128, 128, "zx"),
    ("p", 48, 512, "xz"),
    ("o", 48, 384, "zx"),
    ("a0", 48, 256, "xz"),
    ("b0", 48, 128, "zx"),
    ("a1", 48, 256, "zx"),
    ("b1", 48, 128, "xz"),
    ("a2", 48, 256, "xz"),
    ("b2", 48, 128, "zx"),
    ("g", 16, 128, "zx"),
)
N_ITEMS = len(ITEMS)
INDEX = {item[0]: i for i, item in enumerate(ITEMS)}


def remote(src, dst, sems, index, where):
    return pltpu.make_async_remote_copy(
        src_ref=src,
        dst_ref=dst,
        send_sem=sems[0].at[index],
        recv_sem=sems[1].at[index],
        device_id=where,
        device_id_type=MESH,
    )


def step_kernel(
    ev_ref,
    lab_ref,
    cnt_ref,
    gain_ref,
    wqkv_any,
    wout_any,
    wpiece_any,
    table_any,
    rows_ref,
    gain_out,
    qkv_ref,
    out_ref,
    piece_ref,
    tab_ref,
    wqkv,
    wout,
    wpiece,
    table_ref,
    load_sem,
    hot_ref,
    packed,
    landed,
    rows_out,
    returned,
    there_send,
    there_recv,
    back_send,
    back_recv,
    sum_send,
    sum_recv,
    src_t,
    src_p,
    src_o,
    src_a,
    src_b,
    src_g,
    tiles,
    normed,
    normed_t,
    qkv,
    prob,
    ctx,
    hidden,
    reps,
    reps_t,
    greps,
    glow,
    ghid,
    gctx,
    dqkv,
    bias,
    labs,
    gtab_t,
    gnorm,
    *spare,
):
    bufs = [spare[6 * i : 6 * i + 6] for i in range(N_ITEMS)]
    sems = (sum_send, sum_recv)
    me = lax.axis_index("win")
    y = lax.axis_index("rep")
    core = lax.rem(me, 2)
    z_at = lax.rem(me // 2, 4)
    x_at = me // 8

    barrier = pltpu.get_barrier_semaphore()

    @pl.loop(1, WIN)
    def _(k):
        pl.semaphore_signal(
            barrier, inc=1, device_id={"win": lax.rem(me + k, WIN)}, device_id_type=MESH
        )

    @pl.loop(1, 4)
    def _(k):
        pl.semaphore_signal(
            barrier, inc=1, device_id={"rep": lax.rem(y + k, 4)}, device_id_type=MESH
        )

    loads = [
        pltpu.make_async_copy(src, dst, load_sem.at[i])
        for i, (src, dst) in enumerate(
            ((wqkv_any, wqkv), (wout_any, wout), (wpiece_any, wpiece), (table_any, table_ref))
        )
    ]
    for load in loads:
        load.start()

    counts = cnt_ref[...].astype(F32)
    row = lax.broadcasted_iota(jnp.int32, (ROWS, WIN), 0)
    owner = lax.broadcasted_iota(jnp.int32, (ROWS, WIN), 1)
    row_owner = row // SLOT
    mine = jnp.sum(jnp.where(owner == row_owner, counts, 0.0), 1, keepdims=True)
    start = jnp.sum(jnp.where(owner < row_owner, counts, 0.0), 1, keepdims=True)
    offset = (lax.broadcasted_iota(jnp.int32, (ROWS, 1), 0) % SLOT).astype(F32)
    place = lax.broadcasted_iota(jnp.int32, (ROWS, EVENTS), 1).astype(F32)
    wanted = jnp.where(offset < mine, start + offset, -1.0)
    hot = jnp.where(place == wanted, 1.0, 0.0).astype(BF16)
    hot_ref[...] = hot
    packed[:, :, :D] = mm(hot, ev_ref[...]).astype(BF16).reshape(WIN, SLOT, D)

    lab = lab_ref[...]
    high = lab[1:2] // 64
    rows = [lab[0:1], high, lab[1:2] - high * 64, lab[2:3], jnp.maximum(lab[2:3], lab[3:4])]
    rows.append(jnp.ones((1, EVENTS), jnp.int32))
    rows.append(jnp.zeros((2, EVENTS), jnp.int32))
    table = jnp.concatenate(rows, 0).astype(F32)
    table = jnp.concatenate([table, jnp.zeros((LAB - 8, EVENTS), F32)], 0).astype(BF16)
    packed[:, :, D:] = mm_nt(hot, table).astype(BF16).reshape(WIN, SLOT, LAB)

    pl.semaphore_wait(barrier, WIN - 1 + 3)
    exchange_rows(packed, landed, there_send, there_recv, me)
    landed[me] = packed[me]
    wait_rows(packed, landed, there_send, there_recv, me)

    sources = {"t": src_t, "p": src_p, "o": src_o, "g": src_g}
    for s in range(3):
        sources["a%d" % s] = src_a.at[s]
        sources["b%d" % s] = src_b.at[s]

    def place_of(order, step, k):
        return lax.rem((x_at if order[step] == "x" else z_at) + k, 4)

    def win_of(order, step, k):
        if order[step] == "x":
            return lax.rem(x_at + k, 4) * 8 + z_at * 2 + core
        return x_at * 8 + lax.rem(z_at + k, 4) * 2 + core

    def blocked(name):
        _, rows, width, _ = ITEMS[INDEX[name]]
        return sources[name].reshape(4, 4, 2, rows, width)

    def buf(name):
        return bufs[INDEX[name]]

    def core_copy(name):
        i = INDEX[name]
        return remote(
            blocked(name).at[:, :, 1 - core], buf(name)[0], sems, (i, 0), {"win": me + 1 - 2 * core}
        )

    def at_xz(ref, order, first, second=None):
        if order == "xz":
            return ref.at[first] if second is None else ref.at[first, second]
        return ref.at[:, first] if second is None else ref.at[second, first]

    def ring_copy(name, step, k):
        i = INDEX[name]
        order = ITEMS[i][3]
        if step == 0:
            src = at_xz(buf(name)[0], order, place_of(order, 0, k))
        else:
            src = buf(name)[2].at[place_of(order, 1, k)]
        return remote(
            src,
            buf(name)[1 + 2 * step].at[k - 1],
            sems,
            (i, 1 + 3 * step + k - 1),
            {"win": win_of(order, step, k)},
        )

    def last_copy(name, k):
        return remote(
            buf(name)[4].at[lax.rem(y + k, 4)],
            buf(name)[5].at[k - 1],
            sems,
            (INDEX[name], 7 + k - 1),
            {"rep": lax.rem(y + k, 4)},
        )

    def begin(name):
        core_copy(name).start()

    def to_first_ring(name):
        core_copy(name).wait()
        src, got = blocked(name), buf(name)[0]
        for a in range(4):

            @pl.loop(0, 4)
            def _(b):
                got[a, b] = (src[a, b, core].astype(F32) + got[a, b].astype(F32)).astype(BF16)

        for k in (2, 1, 3):
            ring_copy(name, 0, k).start()

    def to_second_ring(name):
        order = ITEMS[INDEX[name]][3]
        for k in (2, 1, 3):
            ring_copy(name, 0, k).wait()
        mine, got, acc = buf(name)[0], buf(name)[1], buf(name)[2]

        @pl.loop(0, 4)
        def _(b):
            total = at_xz(mine, order, place_of(order, 0, 0), b)[...].astype(F32)
            for k in range(3):
                total += got[k, b].astype(F32)
            acc[b] = total.astype(BF16)

        for k in (2, 1, 3):
            ring_copy(name, 1, k).start()

    def to_last(name):
        _, rows, width, order = ITEMS[INDEX[name]]
        for k in (2, 1, 3):
            ring_copy(name, 1, k).wait()
        got = buf(name)[3]
        total = buf(name)[2][place_of(order, 1, 0)].astype(F32)
        for k in range(3):
            total += got[k].astype(F32)
        low = buf(name)[4]
        if name == "t":
            low[...] = total.astype(BF16).reshape(4, 32, 128)
        elif name == "g":
            for yy in range(4):
                low[yy] = (pltpu.roll(total, 128 - 6 * yy, 1) if yy else total).astype(BF16)
        else:
            for half in range(2):
                for t in range(3):
                    at = t * 16 + half * 8
                    tiles[half, t * 8 : t * 8 + 8, :width] = total[at : at + 8]
            for yy in range(4):
                both = jnp.concatenate(
                    [tiles[0, 6 * yy : 6 * yy + 8, :width], tiles[1, 6 * yy : 6 * yy + 8, :width]], 0
                )
                low[yy] = both.astype(BF16)
        for k in (2, 1, 3):
            last_copy(name, k).start()

    def finish(name):
        _, rows, width, order = ITEMS[INDEX[name]]
        for k in (2, 1, 3):
            last_copy(name, k).wait()
        got = buf(name)[5]
        total = buf(name)[4][y].astype(F32)
        for k in range(3):
            total += got[k].astype(F32)
        total = total * (1.0 / math.sqrt(EVENTS * WIN * 4))
        if name == "t":
            tab_ref[...] = total
        elif name == "g":
            gain_out[...] = total[:8]
        else:
            for u in range(width // 128):
                if name == "p":
                    dst, at = piece_ref, u * 256
                elif name == "o":
                    dst, at = out_ref, u * 256
                else:
                    part = u if name[0] == "a" else 2
                    dst, at = qkv_ref, part * D + int(name[1]) * 256
                us = slice(u * 128, u * 128 + 128)
                dst[:, at : at + 128] = total[:6, us]
                dst[:, at + 128 : at + 256] = total[8:14, us]

    gain = gain_ref[...]
    lab = landed[:, :, D:].reshape(ROWS, LAB).astype(F32)
    valid = lab[:, 5:6] > 0.5
    patient = jnp.where(valid, lab[:, 0:1], -1.0)
    labs[0] = jnp.broadcast_to(lab[:, 1:2] * 64.0 + lab[:, 2:3], (ROWS, 128))
    labs[1] = jnp.broadcast_to(jnp.where(valid, lab[:, 3:4], -1.0), (ROWS, 128))
    labs[2] = jnp.broadcast_to(jnp.where(valid, lab[:, 4:5], -1.0), (ROWS, 128))

    lab_t = lab.T
    patient_row = jnp.where(lab_t[5:6] > 0.5, lab_t[0:1], -1.0)
    row = lax.broadcasted_iota(jnp.int32, (ROWS, ROWS), 0)
    col = lax.broadcasted_iota(jnp.int32, (ROWS, ROWS), 1)
    allowed = ((patient == patient_row) & (col <= row)) | (col == row)
    bias[...] = jnp.where(allowed, 0.0, -1e30)

    x = landed[:, :, :D].reshape(ROWS, D).astype(F32)
    inv_rms = lax.rsqrt(jnp.mean(x * x, -1, keepdims=True) + EPSILON)
    normed[...] = (x * inv_rms * gain).astype(BF16)

    loads[0].wait()

    @pl.loop(0, 9)
    def _(j):
        cols = pl.ds(pl.multiple_of(j * 256, 256), 256)
        res = mm(normed[...], wqkv[:, cols])
        scale = jnp.where(j < 3, 0.125, 1.0)
        res = (res * scale).astype(BF16)
        qkv[2 * j] = res[:, :128]
        qkv[2 * j + 1] = res[:, 128:]

    low_lanes = lax.broadcasted_iota(jnp.int32, (1, 128), 1) < 64

    def head_part(value, head):
        zero = jnp.zeros((), value.dtype)
        return jnp.where(low_lanes, value, zero) if head == 0 else jnp.where(low_lanes, zero, value)

    @pl.loop(0, PAIRS)
    def _(p):
        q = qkv[p]
        k = qkv[PAIRS + p]
        v = qkv[2 * PAIRS + p]
        for rb in range(2):
            rs = slice(rb * 256, rb * 256 + 256)
            n = (rb + 1) * 256
            parts = []
            for head in range(2):
                s = mm_nt(head_part(q[rs], head), k[:n]) + bias[rs, :n]
                w = jnp.exp(s - jnp.max(s, -1, keepdims=True))
                pr = (w * (1.0 / jnp.sum(w, -1, keepdims=True))).astype(BF16)
                prob[p, head, rs, :n] = pr
                parts.append(mm(pr, v[:n]))
            ctx[rs, lanes(p)] = jnp.where(low_lanes, parts[0], parts[1]).astype(BF16)

    loads[1].wait()

    @pl.loop(0, 3)
    def _(j):
        cols = pl.ds(pl.multiple_of(j * 256, 256), 256)
        res = mm(ctx[...], wout[:, cols])
        hidden[:, cols] = (landed[:, :, cols].reshape(ROWS, 256).astype(F32) + res).astype(BF16)

    loads[2].wait()

    @pl.loop(0, 4)
    def _(j):
        cols = pl.ds(pl.multiple_of(j * 256, 256), 256)
        res = mm(hidden[...], wpiece[:, cols])
        for i in range(2):
            part = res[:, i * 128 : i * 128 + 128]
            reps[2 * j + i] = part.astype(BF16)
            reps_t[2 * j + i] = part.T.astype(BF16)

    loads[3].wait()
    log_codes = math.log(CODES)
    times = BLOCK // 128

    def widen(tile):
        return jnp.concatenate([tile] * times, 1)

    greps[...] = jnp.zeros_like(greps)

    @pl.loop(0, CODES // BLOCK)
    def _(b):
        codes_at = pl.ds(pl.multiple_of(b * BLOCK, BLOCK), BLOCK)
        tab = table_ref[codes_at, :]
        ids = (b * BLOCK + lax.broadcasted_iota(jnp.int32, (1, BLOCK), 1)).astype(F32)
        gtab_t[:, codes_at] = jnp.zeros((R, BLOCK), F32)

        @pl.loop(0, PIECES)
        def _(p):
            piece = p.astype(F32)
            code, event, end = labs[0], labs[1], labs[2]
            at_row = jnp.where(end >= piece, -log_codes, -1e30)
            at_code = jnp.where(event >= piece, -log_codes, -1e30)
            target = jnp.where(event == piece, 1.0, 0.0)
            logits = mm_nt(reps[p], tab)
            is_code = widen(code) == ids
            e = jnp.exp(logits + jnp.where(is_code, widen(at_code), widen(at_row)))
            g = (e - jnp.where(is_code, widen(target), 0.0)).astype(BF16)
            greps[p] += mm(g, tab)
            gtab_t[:, codes_at] += mm(reps_t[p], g)

        blocks = BLOCK // 128
        turned = gtab_t[:, codes_at].T.astype(BF16).reshape(blocks, 128, 128)
        src_t[pl.ds(b * blocks, blocks)] = turned

    begin("t")

    for p in range(PIECES):
        glow[:, p * 128 : p * 128 + 128] = greps[p].astype(BF16)

    hidden_t = hidden[...].T
    for j in range(4):
        cols = slice(j * 256, j * 256 + 256)
        src_p[:, :, j * 128 : j * 128 + 128] = stack_halves(mm(hidden_t, glow[:, cols]))
    begin("p")

    for j in range(3):
        cols = slice(j * 256, j * 256 + 256)
        ghid[:, cols] = mm_nt(glow[...], wpiece[cols, :]).astype(BF16)

    ctx_t = ctx[...].T
    for j in range(3):
        cols = slice(j * 256, j * 256 + 256)
        src_o[:, :, j * 128 : j * 128 + 128] = stack_halves(mm(ctx_t, ghid[:, cols]))
    begin("o")

    for j in range(3):
        cols = slice(j * 256, j * 256 + 256)
        gctx[:, cols] = mm_nt(ghid[...], wout[cols, :]).astype(BF16)
    normed_t[...] = normed[...].T
    to_first_ring("t")

    def backward_pair(p):
        q = qkv[p]
        k = qkv[PAIRS + p]
        v = qkv[2 * PAIRS + p]
        g = gctx[:, lanes(p)]
        dk = [None, None]
        dv = [None, None]
        for rb in range(2):
            rs = slice(rb * 256, rb * 256 + 256)
            n = (rb + 1) * 256
            dq = []
            for head in range(2):
                gh = head_part(g[rs], head)
                qh = head_part(q[rs], head)
                pr_low = prob[p, head, rs, :n]
                pr = pr_low.astype(F32)
                dp = mm_nt(gh, v[:n])
                inner = jnp.sum(dp * pr, -1, keepdims=True)
                ds = (pr * (dp - inner)).astype(BF16)
                dq.append(mm(ds, k[:n]))
                dv_now = mm_tn(pr_low, gh)
                dk_now = mm_tn(ds, qh)
                for half in range(rb + 1):
                    hs = slice(half * 256, half * 256 + 256)
                    dv[half] = dv_now[hs] if dv[half] is None else dv[half] + dv_now[hs]
                    dk[half] = dk_now[hs] if dk[half] is None else dk[half] + dk_now[hs]
            dqkv[rs, lanes(p)] = (jnp.where(low_lanes, dq[0], dq[1]) * 0.125).astype(BF16)
        for half in range(2):
            hs = slice(half * 256, half * 256 + 256)
            dqkv[hs, lanes(PAIRS + p)] = dk[half].astype(BF16)
            dqkv[hs, lanes(2 * PAIRS + p)] = dv[half].astype(BF16)

    def backward_step(s):
        pl.loop(2 * s, 2 * s + 2)(backward_pair)

    def qkv_step(s):
        for part in range(3):
            cols = slice(part * D + s * 256, part * D + s * 256 + 256)
            res = stack_halves(mm(normed_t[...], dqkv[:, cols]))
            if part < 2:
                src_a[s, :, :, part * 128 : part * 128 + 128] = res
            else:
                src_b[s] = res
        begin("a%d" % s)
        begin("b%d" % s)

    backward_step(0)
    to_first_ring("p")
    to_first_ring("o")
    qkv_step(0)
    to_second_ring("t")
    backward_step(1)
    to_first_ring("a0")
    to_first_ring("b0")
    qkv_step(1)
    to_second_ring("p")
    to_second_ring("o")
    to_last("t")
    backward_step(2)
    to_first_ring("a1")
    to_first_ring("b1")
    qkv_step(2)
    to_second_ring("a0")
    to_second_ring("b0")

    for j in range(3):
        cols = slice(j * 256, j * 256 + 256)
        gnorm[:, cols] = mm_nt(dqkv[...], wqkv[cols, :])

    x = landed[:, :, :D].reshape(ROWS, D).astype(F32)
    inv_rms = lax.rsqrt(jnp.mean(x * x, -1, keepdims=True) + EPSILON)
    x_hat = x * inv_rms
    gn = gnorm[...]
    ggain = jnp.sum(gn * x_hat, 0, keepdims=True)
    gh = gn * gain
    gx = inv_rms * (gh - x_hat * jnp.mean(gh * x_hat, -1, keepdims=True))
    gb = (gx + ghid[...].astype(F32)).astype(BF16)
    rows_out[...] = gb.reshape(WIN, SLOT, D)

    exchange_rows(rows_out, returned, back_send, back_recv, me)
    returned[me] = rows_out[me]

    feature = lax.broadcasted_iota(jnp.int32, (ROWS, D), 1)
    block = lax.broadcasted_iota(jnp.int32, (ROWS, D), 0) // SLOT
    spread = jnp.where(feature // 24 == block, ggain, 0.0).astype(BF16)
    pick = lax.broadcasted_iota(jnp.int32, (D, 128), 0) % 24
    pick = jnp.where(pick == lax.broadcasted_iota(jnp.int32, (D, 128), 1), 1.0, 0.0).astype(BF16)
    src_g[...] = mm(spread, pick).astype(BF16).reshape(WIN, SLOT, 128)
    begin("g")
    to_first_ring("a2")
    to_first_ring("b2")
    to_second_ring("a1")
    to_second_ring("b1")
    to_last("p")
    to_last("o")
    to_first_ring("g")
    to_last("a0")
    to_last("b0")
    to_second_ring("a2")
    to_second_ring("b2")
    to_last("a1")
    to_last("b1")
    to_second_ring("g")
    to_last("a2")
    to_last("b2")
    to_last("g")
    for name in ("t", "p", "o", "a0", "b0", "a1", "b1"):
        finish(name)
    wait_rows(rows_out, returned, back_send, back_recv, me)
    rows_ref[...] = mm_tn(hot_ref[...], returned[...].reshape(ROWS, D)).astype(BF16)
    for name in ("a2", "b2", "g"):
        finish(name)


def step(events, labels, counts, gain, w_qkv, w_out, w_piece, table):
    vmem = pl.BlockSpec(memory_space=pltpu.VMEM)
    scratch = [
        pltpu.VMEM((D, 3 * D), BF16),
        pltpu.VMEM((D, D), BF16),
        pltpu.VMEM((D, PIECES * R), BF16),
        pltpu.VMEM((CODES, R), BF16),
        pltpu.SemaphoreType.DMA((4,)),
        pltpu.VMEM((ROWS, EVENTS), BF16),
        pltpu.VMEM((WIN, SLOT, WIDE), BF16),
        pltpu.VMEM((WIN, SLOT, WIDE), BF16),
        pltpu.VMEM((WIN, SLOT, D), BF16),
        pltpu.VMEM((WIN, SLOT, D), BF16),
        pltpu.SemaphoreType.DMA((WIN,)),
        pltpu.SemaphoreType.DMA((WIN,)),
        pltpu.SemaphoreType.DMA((WIN,)),
        pltpu.SemaphoreType.DMA((WIN,)),
        pltpu.SemaphoreType.DMA((N_ITEMS, 10)),
        pltpu.SemaphoreType.DMA((N_ITEMS, 10)),
        pltpu.VMEM((WIN, 128, 128), BF16),
        pltpu.VMEM((WIN, 48, 512), BF16),
        pltpu.VMEM((WIN, 48, 384), BF16),
        pltpu.VMEM((3, WIN, 48, 256), BF16),
        pltpu.VMEM((3, WIN, 48, 128), BF16),
        pltpu.VMEM((WIN, SLOT, 128), BF16),
        pltpu.VMEM((2, 32, 512), F32),
        pltpu.VMEM((ROWS, D), BF16),
        pltpu.VMEM((D, ROWS), BF16),
        pltpu.VMEM((18, ROWS, 128), BF16),
        pltpu.VMEM((PAIRS, 2, ROWS, ROWS), BF16),
        pltpu.VMEM((ROWS, D), BF16),
        pltpu.VMEM((ROWS, D), BF16),
        pltpu.VMEM((PIECES, ROWS, R), BF16),
        pltpu.VMEM((PIECES, R, ROWS), BF16),
        pltpu.VMEM((PIECES, ROWS, R), F32),
        pltpu.VMEM((ROWS, PIECES * R), BF16),
        pltpu.VMEM((ROWS, D), BF16),
        pltpu.VMEM((ROWS, D), BF16),
        pltpu.VMEM((ROWS, 3 * D), BF16),
        pltpu.VMEM((ROWS, ROWS), F32),
        pltpu.VMEM((3, ROWS, 128), F32),
        pltpu.VMEM((R, CODES), F32),
        pltpu.VMEM((ROWS, D), F32),
    ]
    for name, rows, width, order in ITEMS:
        last = 32 if name == "t" else 16
        scratch += [
            pltpu.VMEM((4, 4, rows, width), BF16),
            pltpu.VMEM((3, 4, rows, width), BF16),
            pltpu.VMEM((4, rows, width), BF16),
            pltpu.VMEM((3, rows, width), BF16),
            pltpu.VMEM((4, last, width), BF16),
            pltpu.VMEM((3, last, width), BF16),
        ]
    return pl.pallas_call(
        step_kernel,
        out_shape=(
            jax.ShapeDtypeStruct((EVENTS, D), BF16),
            jax.ShapeDtypeStruct((8, 128), F32),
            jax.ShapeDtypeStruct((6, 3 * D), F32),
            jax.ShapeDtypeStruct((6, D), F32),
            jax.ShapeDtypeStruct((6, PIECES * R), F32),
            jax.ShapeDtypeStruct((32, R), F32),
        ),
        in_specs=[vmem] * 4 + [pl.BlockSpec(memory_space=pl.ANY)] * 4,
        out_specs=(vmem,) * 6,
        scratch_shapes=scratch,
        compiler_params=pltpu.CompilerParams(
            collective_id=1, has_side_effects=True, vmem_limit_bytes=62 * 1024 * 1024
        ),
        name="step",
    )(events, labels, counts, gain, w_qkv, w_out, w_piece, table)


def result_kernel(*refs):
    for src, dst in zip(refs[:5], refs[6:11]):
        dst[...] = src[...]
    refs[11][...] = refs[5][0, :6]


def results(rows, g_qkv, g_out, g_piece, g_table, gain):
    vmem = pl.BlockSpec(memory_space=pltpu.VMEM)
    like = [jax.ShapeDtypeStruct(a.shape, a.dtype) for a in (rows, g_qkv, g_out, g_piece, g_table)]
    return pl.pallas_call(
        result_kernel,
        out_shape=(*like, jax.ShapeDtypeStruct((6,), F32)),
        in_specs=[vmem] * 6,
        out_specs=(vmem,) * 6,
        name="results",
    )(rows, g_qkv, g_out, g_piece, g_table, gain)


def body(
    events,
    send_counts,
    patient_ids,
    codes,
    event_piece,
    censor_piece,
    norm_gain,
    w_qkv,
    w_out,
    w_piece,
    code_table,
):
    labels = jnp.concatenate([patient_ids[0], codes[0], event_piece[0], censor_piece[0]], 0)
    rows, gain, g_qkv, g_out, g_piece, g_table = step(
        events[0, 0], labels, send_counts[0], norm_gain[None], w_qkv, w_out, w_piece, code_table
    )
    rows, g_qkv, g_out, g_piece, g_table, g_gain = results(rows, g_qkv, g_out, g_piece, g_table, gain)
    return (rows[None, None], g_gain, g_qkv, g_out, g_piece, g_table)


def solution(mesh):
    split = P("win", "rep")
    return jax.shard_map(
        body,
        mesh=mesh,
        in_specs=(split,) * 6 + (P(),) * 5,
        out_specs=(split,) + (P(("win", "rep")),) * 5,
        check_vma=False,
    )
```

```python
import functools
import math

import jax
import jax.numpy as jnp
from jax import lax
from jax.experimental import pallas as pl
from jax.experimental.pallas import tpu as pltpu
from jax.sharding import PartitionSpec as P

HEADS = 12
EPSILON = 1e-05
MESH = pl.DeviceIdType.MESH

D = 768
PAIRS = 6
PIECES = 8
CODES = 4096
R = 128
ROWS = 512
EVENTS = 256
WIN = 32
SLOT = 16
LAB = 128
WIDE = D + LAB
BLOCK = 1024
LOG2E = math.log2(math.e)

F32 = jnp.float32
BF16 = jnp.bfloat16

NT = (((1,), (1,)), ((), ()))
TN = (((0,), (0,)), ((), ()))


def mm(a, b):
    return jnp.dot(a, b, preferred_element_type=F32)


def mm_nt(a, b):
    return lax.dot_general(a, b, NT, preferred_element_type=F32)


def mm_tn(a, b):
    return lax.dot_general(a, b, TN, preferred_element_type=F32)


def exchange_rows(src_ref, dst_ref, send_sem, recv_sem, me):
    @pl.loop(1, WIN)
    def _(k):
        peer = lax.rem(me + k, WIN)
        pltpu.make_async_remote_copy(
            src_ref=src_ref.at[peer],
            dst_ref=dst_ref.at[me],
            send_sem=send_sem.at[k],
            recv_sem=recv_sem.at[k],
            device_id={"win": peer},
            device_id_type=MESH,
        ).start()


def wait_rows(src_ref, dst_ref, send_sem, recv_sem, me):
    @pl.loop(1, WIN)
    def _(k):
        sender = lax.rem(me + WIN - k, WIN)
        pltpu.make_async_remote_copy(
            src_ref=src_ref.at[me],
            dst_ref=dst_ref.at[sender],
            send_sem=send_sem.at[k],
            recv_sem=recv_sem.at[k],
            device_id={"win": sender},
            device_id_type=MESH,
        ).wait()


def stack_halves(res):
    tiles = res.reshape(WIN, 3, 8, 256)
    both = jnp.concatenate([tiles[..., :128], tiles[..., 128:]], 2)
    return both.reshape(WIN, 48, 128).astype(BF16)


TODO = [(rb, head) for rb in range(2) for head in range(2)]


def span(rb):
    return slice(rb * 256, rb * 256 + 256)


def far(rb):
    return rb * 256 + 256


def lanes(index):
    return pl.ds(pl.multiple_of(index * 128, 128), 128)


ITEMS = (
    ("t", 128, 128, "zx"),
    ("p", 48, 512, "xz"),
    ("o", 48, 384, "zx"),
    ("a0", 48, 256, "xz"),
    ("b0", 48, 128, "zx"),
    ("a1", 48, 256, "zx"),
    ("b1", 48, 128, "xz"),
    ("a2", 48, 256, "xz"),
    ("b2", 48, 128, "zx"),
    ("g", 16, 128, "zx"),
)
N_ITEMS = len(ITEMS)
INDEX = {item[0]: i for i, item in enumerate(ITEMS)}


def remote(src, dst, sems, index, where):
    return pltpu.make_async_remote_copy(
        src_ref=src,
        dst_ref=dst,
        send_sem=sems[0].at[index],
        recv_sem=sems[1].at[index],
        device_id=where,
        device_id_type=MESH,
    )


def step_kernel(
    ev_ref,
    lab_ref,
    cnt_ref,
    gain_ref,
    wqkv_any,
    wout_any,
    wpiece_any,
    table_any,
    rows_ref,
    gain_out,
    qkv_ref,
    out_ref,
    piece_ref,
    tab_ref,
    wqkv,
    wout,
    wpiece,
    table_ref,
    load_sem,
    hot_ref,
    packed,
    landed,
    rows_out,
    returned,
    there_send,
    there_recv,
    back_send,
    back_recv,
    sum_send,
    sum_recv,
    src_t,
    src_p,
    src_o,
    src_a,
    src_b,
    src_g,
    tiles,
    normed,
    normed_t,
    qkv,
    prob,
    ctx,
    hidden,
    reps,
    reps_t,
    greps,
    own_row,
    fix,
    glow,
    ghid,
    gctx,
    dqkv,
    bias,
    labs,
    gnorm,
    *spare,
):
    bufs = [spare[6 * i : 6 * i + 6] for i in range(N_ITEMS)]
    sems = (sum_send, sum_recv)
    me = lax.axis_index("win")
    y = lax.axis_index("rep")
    core = lax.rem(me, 2)
    z_at = lax.rem(me // 2, 4)
    x_at = me // 8

    barrier = pltpu.get_barrier_semaphore()

    @pl.loop(1, WIN)
    def _(k):
        pl.semaphore_signal(
            barrier, inc=1, device_id={"win": lax.rem(me + k, WIN)}, device_id_type=MESH
        )

    @pl.loop(1, 4)
    def _(k):
        pl.semaphore_signal(
            barrier, inc=1, device_id={"rep": lax.rem(y + k, 4)}, device_id_type=MESH
        )

    loads = [
        pltpu.make_async_copy(src, dst, load_sem.at[i])
        for i, (src, dst) in enumerate(
            ((wqkv_any, wqkv), (wout_any, wout), (wpiece_any, wpiece), (table_any, table_ref))
        )
    ]
    for load in loads:
        load.start()

    counts = cnt_ref[...].astype(F32)
    row = lax.broadcasted_iota(jnp.int32, (ROWS, WIN), 0)
    owner = lax.broadcasted_iota(jnp.int32, (ROWS, WIN), 1)
    row_owner = row // SLOT
    mine = jnp.sum(jnp.where(owner == row_owner, counts, 0.0), 1, keepdims=True)
    start = jnp.sum(jnp.where(owner < row_owner, counts, 0.0), 1, keepdims=True)
    offset = (lax.broadcasted_iota(jnp.int32, (ROWS, 1), 0) % SLOT).astype(F32)
    place = lax.broadcasted_iota(jnp.int32, (ROWS, EVENTS), 1).astype(F32)
    wanted = jnp.where(offset < mine, start + offset, -1.0)
    hot = jnp.where(place == wanted, 1.0, 0.0).astype(BF16)
    hot_ref[...] = hot
    packed[:, :, :D] = mm(hot, ev_ref[...]).astype(BF16).reshape(WIN, SLOT, D)

    lab = lab_ref[...]
    high = lab[1:2] // 64
    rows = [lab[0:1], high, lab[1:2] - high * 64, lab[2:3], jnp.maximum(lab[2:3], lab[3:4])]
    rows.append(jnp.ones((1, EVENTS), jnp.int32))
    rows.append(jnp.zeros((2, EVENTS), jnp.int32))
    table = jnp.concatenate(rows, 0).astype(F32)
    table = jnp.concatenate([table, jnp.zeros((LAB - 8, EVENTS), F32)], 0).astype(BF16)
    packed[:, :, D:] = mm_nt(hot, table).astype(BF16).reshape(WIN, SLOT, LAB)

    pl.semaphore_wait(barrier, WIN - 1 + 3)
    exchange_rows(packed, landed, there_send, there_recv, me)
    landed[me] = packed[me]
    wait_rows(packed, landed, there_send, there_recv, me)

    sources = {"t": src_t, "p": src_p, "o": src_o, "g": src_g}
    for s in range(3):
        sources["a%d" % s] = src_a.at[s]
        sources["b%d" % s] = src_b.at[s]

    def place_of(order, step, k):
        return lax.rem((x_at if order[step] == "x" else z_at) + k, 4)

    def win_of(order, step, k):
        if order[step] == "x":
            return lax.rem(x_at + k, 4) * 8 + z_at * 2 + core
        return x_at * 8 + lax.rem(z_at + k, 4) * 2 + core

    def blocked(name):
        _, rows, width, _ = ITEMS[INDEX[name]]
        return sources[name].reshape(4, 4, 2, rows, width)

    def buf(name):
        return bufs[INDEX[name]]

    def core_copy(name):
        i = INDEX[name]
        return remote(
            blocked(name).at[:, :, 1 - core], buf(name)[0], sems, (i, 0), {"win": me + 1 - 2 * core}
        )

    def at_xz(ref, order, first, second=None):
        if order == "xz":
            return ref.at[first] if second is None else ref.at[first, second]
        return ref.at[:, first] if second is None else ref.at[second, first]

    def ring_copy(name, step, k):
        i = INDEX[name]
        order = ITEMS[i][3]
        if step == 0:
            src = at_xz(buf(name)[0], order, place_of(order, 0, k))
        else:
            src = buf(name)[2].at[place_of(order, 1, k)]
        return remote(
            src,
            buf(name)[1 + 2 * step].at[k - 1],
            sems,
            (i, 1 + 3 * step + k - 1),
            {"win": win_of(order, step, k)},
        )

    def last_copy(name, k):
        return remote(
            buf(name)[4].at[lax.rem(y + k, 4)],
            buf(name)[5].at[k - 1],
            sems,
            (INDEX[name], 7 + k - 1),
            {"rep": lax.rem(y + k, 4)},
        )

    def begin(name):
        core_copy(name).start()

    def to_first_ring(name):
        core_copy(name).wait()
        src, got = blocked(name), buf(name)[0]
        for a in range(4):

            @pl.loop(0, 4)
            def _(b):
                got[a, b] = (src[a, b, core].astype(F32) + got[a, b].astype(F32)).astype(BF16)

        for k in (2, 1, 3):
            ring_copy(name, 0, k).start()

    def to_second_ring(name):
        order = ITEMS[INDEX[name]][3]
        for k in (2, 1, 3):
            ring_copy(name, 0, k).wait()
        mine, got, acc = buf(name)[0], buf(name)[1], buf(name)[2]

        @pl.loop(0, 4)
        def _(b):
            total = at_xz(mine, order, place_of(order, 0, 0), b)[...].astype(F32)
            for k in range(3):
                total += got[k, b].astype(F32)
            acc[b] = total.astype(BF16)

        for k in (2, 1, 3):
            ring_copy(name, 1, k).start()

    def to_last(name):
        _, rows, width, order = ITEMS[INDEX[name]]
        for k in (2, 1, 3):
            ring_copy(name, 1, k).wait()
        got = buf(name)[3]
        total = buf(name)[2][place_of(order, 1, 0)].astype(F32)
        for k in range(3):
            total += got[k].astype(F32)
        low = buf(name)[4]
        if name == "t":
            low[...] = total.astype(BF16).reshape(4, 32, 128)
        elif name == "g":
            for yy in range(4):
                low[yy] = (pltpu.roll(total, 128 - 6 * yy, 1) if yy else total).astype(BF16)
        else:
            for half in range(2):
                for t in range(3):
                    at = t * 16 + half * 8
                    tiles[half, t * 8 : t * 8 + 8, :width] = total[at : at + 8]
            for yy in range(4):
                both = jnp.concatenate(
                    [tiles[0, 6 * yy : 6 * yy + 8, :width], tiles[1, 6 * yy : 6 * yy + 8, :width]], 0
                )
                low[yy] = both.astype(BF16)
        for k in (2, 1, 3):
            last_copy(name, k).start()

    def finish(name):
        _, rows, width, order = ITEMS[INDEX[name]]
        for k in (2, 1, 3):
            last_copy(name, k).wait()
        got = buf(name)[5]
        total = buf(name)[4][y].astype(F32)
        for k in range(3):
            total += got[k].astype(F32)
        total = total * (1.0 / math.sqrt(EVENTS * WIN * 4))
        if name == "t":
            tab_ref[...] = total
        elif name == "g":
            gain_out[...] = total[:8]
        else:
            for u in range(width // 128):
                if name == "p":
                    dst, at = piece_ref, u * 256
                elif name == "o":
                    dst, at = out_ref, u * 256
                else:
                    part = u if name[0] == "a" else 2
                    dst, at = qkv_ref, part * D + int(name[1]) * 256
                us = slice(u * 128, u * 128 + 128)
                dst[:, at : at + 128] = total[:6, us]
                dst[:, at + 128 : at + 256] = total[8:14, us]

    gain = gain_ref[...]
    lab = landed[:, :, D:].reshape(ROWS, LAB).astype(F32)
    valid = lab[:, 5:6] > 0.5
    patient = jnp.where(valid, lab[:, 0:1], -1.0)
    labs[0] = jnp.broadcast_to(lab[:, 1:2] * 64.0 + lab[:, 2:3], (ROWS, 128))
    labs[1] = jnp.broadcast_to(jnp.where(valid, lab[:, 3:4], -1.0), (ROWS, 128))
    labs[2] = jnp.broadcast_to(jnp.where(valid, lab[:, 4:5], -1.0), (ROWS, 128))

    lab_t = lab.T
    patient_row = jnp.where(lab_t[5:6] > 0.5, lab_t[0:1], -1.0)
    row = lax.broadcasted_iota(jnp.int32, (ROWS, ROWS), 0)
    col = lax.broadcasted_iota(jnp.int32, (ROWS, ROWS), 1)
    allowed = ((patient == patient_row) & (col <= row)) | (col == row)
    bias[...] = jnp.where(allowed, 0.0, -1e30)

    x = landed[:, :, :D].reshape(ROWS, D).astype(F32)
    inv_rms = lax.rsqrt(jnp.mean(x * x, -1, keepdims=True) + EPSILON)
    normed[...] = (x * inv_rms * gain).astype(BF16)

    loads[0].wait()

    @pl.loop(0, 9)
    def _(j):
        cols = pl.ds(pl.multiple_of(j * 256, 256), 256)
        res = mm(normed[...], wqkv[:, cols])
        scale = jnp.where(j < 3, 0.125, 1.0)
        res = (res * scale).astype(BF16)
        qkv[2 * j] = res[:, :128]
        qkv[2 * j + 1] = res[:, 128:]

    low_lanes = lax.broadcasted_iota(jnp.int32, (1, 128), 1) < 64

    def head_part(value, head):
        zero = jnp.zeros((), value.dtype)
        return jnp.where(low_lanes, value, zero) if head == 0 else jnp.where(low_lanes, zero, value)

    @pl.loop(0, PAIRS, unroll=2)
    def _(p):
        q = qkv[p]
        k = qkv[PAIRS + p]
        v = qkv[2 * PAIRS + p]
        s = [mm_nt(head_part(q[span(rb)], head), k[: far(rb)]) + bias[span(rb), : far(rb)] for rb, head in TODO]
        top = [jnp.max(a, -1, keepdims=True) for a in s]
        w = [jnp.exp(a - m) for a, m in zip(s, top)]
        inv = [1.0 / jnp.sum(a, -1, keepdims=True) for a in w]
        pr = [(a * i).astype(BF16) for a, i in zip(w, inv)]
        for (rb, head), a in zip(TODO, pr):
            prob[p, head, span(rb), : far(rb)] = a
        got = [mm(a, v[: far(rb)]) for (rb, head), a in zip(TODO, pr)]
        for rb in range(2):
            ctx[span(rb), lanes(p)] = jnp.where(low_lanes, got[2 * rb], got[2 * rb + 1]).astype(BF16)

    loads[1].wait()

    @pl.loop(0, 3)
    def _(j):
        cols = pl.ds(pl.multiple_of(j * 256, 256), 256)
        res = mm(ctx[...], wout[:, cols])
        hidden[:, cols] = (landed[:, :, cols].reshape(ROWS, 256).astype(F32) + res).astype(BF16)

    loads[2].wait()

    @pl.loop(0, 4)
    def _(j):
        cols = pl.ds(pl.multiple_of(j * 256, 256), 256)
        res = mm(hidden[...], wpiece[:, cols])
        for i in range(2):
            part = res[:, i * 128 : i * 128 + 128]
            reps[2 * j + i] = part.astype(BF16)
            reps_t[2 * j + i] = part.T.astype(BF16)

    loads[3].wait()

    log_codes = math.log2(CODES)
    times = BLOCK // 128
    code, event, end = labs[0], labs[1], labs[2]
    own_code = jnp.where(event >= 0, code, -1.0)

    def widen(tile):
        return jnp.concatenate([tile] * times, 1)

    def block_ids(b):
        return (b * BLOCK + lax.broadcasted_iota(jnp.int32, (1, BLOCK), 1)).astype(F32)

    def block_at(b):
        return pl.ds(pl.multiple_of(b * BLOCK, BLOCK), BLOCK)

    own_row[...] = jnp.zeros_like(own_row)

    @pl.loop(0, CODES // BLOCK)
    def _(b):
        hot = jnp.where(widen(own_code) == block_ids(b), 1.0, 0.0).astype(BF16)
        own_row[...] += mm(hot, table_ref[block_at(b), :])

    for p in range(PIECES):
        at_code = jnp.sum(reps[p].astype(F32) * own_row[...], -1, keepdims=True)
        value = jnp.exp2(at_code * LOG2E - log_codes) - 1.0
        fix[p] = jnp.where(event == p, value, 0.0)

    greps[...] = jnp.zeros_like(greps)

    @pl.loop(0, CODES // BLOCK)
    def _(b):
        tab = table_ref[block_at(b), :]
        ids = block_ids(b)

        def weights(p, logits):
            live = widen(jnp.where(end >= p, -log_codes, -1e30))
            e = jnp.exp2(logits * LOG2E + live)
            act = widen(jnp.where(event <= p, own_code, -1.0))
            return jnp.where(act == ids, widen(fix[p]), e).astype(BF16)

        logits = mm_nt(reps[0], tab)
        total = jnp.zeros((R, BLOCK), F32)
        for p in range(PIECES):
            after = mm_nt(reps[p + 1], tab) if p + 1 < PIECES else None
            g = weights(p, logits)
            greps[p] += mm(g, tab)
            total = total + mm(reps_t[p], g)
            logits = after
        turned = total.T.astype(BF16).reshape(BLOCK // 128, 128, 128)
        src_t[pl.ds(b * (BLOCK // 128), BLOCK // 128)] = turned

    begin("t")

    for p in range(PIECES):
        glow[:, p * 128 : p * 128 + 128] = greps[p].astype(BF16)

    hidden_t = hidden[...].T
    for j in range(4):
        cols = slice(j * 256, j * 256 + 256)
        src_p[:, :, j * 128 : j * 128 + 128] = stack_halves(mm(hidden_t, glow[:, cols]))
    begin("p")

    for j in range(3):
        cols = slice(j * 256, j * 256 + 256)
        ghid[:, cols] = mm_nt(glow[...], wpiece[cols, :]).astype(BF16)

    ctx_t = ctx[...].T
    for j in range(3):
        cols = slice(j * 256, j * 256 + 256)
        src_o[:, :, j * 128 : j * 128 + 128] = stack_halves(mm(ctx_t, ghid[:, cols]))
    begin("o")

    for j in range(3):
        cols = slice(j * 256, j * 256 + 256)
        gctx[:, cols] = mm_nt(ghid[...], wout[cols, :]).astype(BF16)
    normed_t[...] = normed[...].T
    to_first_ring("t")

    def backward_pair(p):
        q = qkv[p]
        k = qkv[PAIRS + p]
        v = qkv[2 * PAIRS + p]
        g = gctx[:, lanes(p)]
        gh = [head_part(g[span(rb)], head) for rb, head in TODO]
        low = [prob[p, head, span(rb), : far(rb)] for rb, head in TODO]
        dp = [mm_nt(a, v[: far(rb)]) for (rb, head), a in zip(TODO, gh)]
        inner = [jnp.sum(a * b.astype(F32), -1, keepdims=True) for a, b in zip(dp, low)]
        ds = [(b.astype(F32) * (a - i)).astype(BF16) for a, b, i in zip(dp, low, inner)]
        cat = lambda a, i: jnp.concatenate([a[i], a[i + 1]], 0)
        dv = [mm_tn(cat(low, i), cat(gh, i)) for i in (0, 2)]
        dq = [mm(a, k[: far(rb)]) for (rb, head), a in zip(TODO, ds)]
        qh = [head_part(q[span(rb)], head) for rb, head in TODO]
        dk = [mm_tn(cat(ds, i), cat(qh, i)) for i in (0, 2)]
        for rb in range(2):
            both = jnp.where(low_lanes, dq[2 * rb], dq[2 * rb + 1]) * 0.125
            dqkv[span(rb), lanes(p)] = both.astype(BF16)
        for at, parts in ((PAIRS, dk), (2 * PAIRS, dv)):
            wide = parts[1]
            dqkv[:256, lanes(at + p)] = (wide[:256] + parts[0]).astype(BF16)
            dqkv[256:, lanes(at + p)] = wide[256:].astype(BF16)

    def backward_step(s):
        pl.loop(2 * s, 2 * s + 2, unroll=2)(backward_pair)

    def qkv_step(s):
        for part in range(3):
            cols = slice(part * D + s * 256, part * D + s * 256 + 256)
            res = stack_halves(mm(normed_t[...], dqkv[:, cols]))
            if part < 2:
                src_a[s, :, :, part * 128 : part * 128 + 128] = res
            else:
                src_b[s] = res
        begin("a%d" % s)
        begin("b%d" % s)

    backward_step(0)
    to_first_ring("p")
    to_first_ring("o")
    qkv_step(0)
    to_second_ring("t")
    backward_step(1)
    to_first_ring("a0")
    to_first_ring("b0")
    qkv_step(1)
    to_second_ring("p")
    to_second_ring("o")
    to_last("t")
    backward_step(2)
    to_first_ring("a1")
    to_first_ring("b1")
    qkv_step(2)
    to_second_ring("a0")
    to_second_ring("b0")

    for j in range(3):
        cols = slice(j * 256, j * 256 + 256)
        gnorm[:, cols] = mm_nt(dqkv[...], wqkv[cols, :])

    x = landed[:, :, :D].reshape(ROWS, D).astype(F32)
    inv_rms = lax.rsqrt(jnp.mean(x * x, -1, keepdims=True) + EPSILON)
    x_hat = x * inv_rms
    gn = gnorm[...]
    ggain = jnp.sum(gn * x_hat, 0, keepdims=True)
    gh = gn * gain
    gx = inv_rms * (gh - x_hat * jnp.mean(gh * x_hat, -1, keepdims=True))
    gb = (gx + ghid[...].astype(F32)).astype(BF16)
    rows_out[...] = gb.reshape(WIN, SLOT, D)

    exchange_rows(rows_out, returned, back_send, back_recv, me)
    returned[me] = rows_out[me]

    feature = lax.broadcasted_iota(jnp.int32, (ROWS, D), 1)
    block = lax.broadcasted_iota(jnp.int32, (ROWS, D), 0) // SLOT
    spread = jnp.where(feature // 24 == block, ggain, 0.0).astype(BF16)
    pick = lax.broadcasted_iota(jnp.int32, (D, 128), 0) % 24
    pick = jnp.where(pick == lax.broadcasted_iota(jnp.int32, (D, 128), 1), 1.0, 0.0).astype(BF16)
    src_g[...] = mm(spread, pick).astype(BF16).reshape(WIN, SLOT, 128)
    begin("g")
    to_first_ring("a2")
    to_first_ring("b2")
    to_second_ring("a1")
    to_second_ring("b1")
    to_last("p")
    to_last("o")
    to_first_ring("g")
    to_last("a0")
    to_last("b0")
    to_second_ring("a2")
    to_second_ring("b2")
    to_last("a1")
    to_last("b1")
    to_second_ring("g")
    to_last("a2")
    to_last("b2")
    to_last("g")
    for name in ("t", "p", "o", "a0", "b0", "a1", "b1"):
        finish(name)
    wait_rows(rows_out, returned, back_send, back_recv, me)
    rows_ref[...] = mm_tn(hot_ref[...], returned[...].reshape(ROWS, D)).astype(BF16)
    for name in ("a2", "b2", "g"):
        finish(name)


def step(events, labels, counts, gain, w_qkv, w_out, w_piece, table):
    vmem = pl.BlockSpec(memory_space=pltpu.VMEM)
    scratch = [
        pltpu.VMEM((D, 3 * D), BF16),
        pltpu.VMEM((D, D), BF16),
        pltpu.VMEM((D, PIECES * R), BF16),
        pltpu.VMEM((CODES, R), BF16),
        pltpu.SemaphoreType.DMA((4,)),
        pltpu.VMEM((ROWS, EVENTS), BF16),
        pltpu.VMEM((WIN, SLOT, WIDE), BF16),
        pltpu.VMEM((WIN, SLOT, WIDE), BF16),
        pltpu.VMEM((WIN, SLOT, D), BF16),
        pltpu.VMEM((WIN, SLOT, D), BF16),
        pltpu.SemaphoreType.DMA((WIN,)),
        pltpu.SemaphoreType.DMA((WIN,)),
        pltpu.SemaphoreType.DMA((WIN,)),
        pltpu.SemaphoreType.DMA((WIN,)),
        pltpu.SemaphoreType.DMA((N_ITEMS, 10)),
        pltpu.SemaphoreType.DMA((N_ITEMS, 10)),
        pltpu.VMEM((WIN, 128, 128), BF16),
        pltpu.VMEM((WIN, 48, 512), BF16),
        pltpu.VMEM((WIN, 48, 384), BF16),
        pltpu.VMEM((3, WIN, 48, 256), BF16),
        pltpu.VMEM((3, WIN, 48, 128), BF16),
        pltpu.VMEM((WIN, SLOT, 128), BF16),
        pltpu.VMEM((2, 32, 512), F32),
        pltpu.VMEM((ROWS, D), BF16),
        pltpu.VMEM((D, ROWS), BF16),
        pltpu.VMEM((18, ROWS, 128), BF16),
        pltpu.VMEM((PAIRS, 2, ROWS, ROWS), BF16),
        pltpu.VMEM((ROWS, D), BF16),
        pltpu.VMEM((ROWS, D), BF16),
        pltpu.VMEM((PIECES, ROWS, R), BF16),
        pltpu.VMEM((PIECES, R, ROWS), BF16),
        pltpu.VMEM((PIECES, ROWS, R), F32),
        pltpu.VMEM((ROWS, R), F32),
        pltpu.VMEM((PIECES, ROWS, 128), F32),
        pltpu.VMEM((ROWS, PIECES * R), BF16),
        pltpu.VMEM((ROWS, D), BF16),
        pltpu.VMEM((ROWS, D), BF16),
        pltpu.VMEM((ROWS, 3 * D), BF16),
        pltpu.VMEM((ROWS, ROWS), F32),
        pltpu.VMEM((3, ROWS, 128), F32),
        pltpu.VMEM((ROWS, D), F32),
    ]
    for name, rows, width, order in ITEMS:
        last = 32 if name == "t" else 16
        scratch += [
            pltpu.VMEM((4, 4, rows, width), BF16),
            pltpu.VMEM((3, 4, rows, width), BF16),
            pltpu.VMEM((4, rows, width), BF16),
            pltpu.VMEM((3, rows, width), BF16),
            pltpu.VMEM((4, last, width), BF16),
            pltpu.VMEM((3, last, width), BF16),
        ]
    return pl.pallas_call(
        step_kernel,
        out_shape=(
            jax.ShapeDtypeStruct((EVENTS, D), BF16),
            jax.ShapeDtypeStruct((8, 128), F32),
            jax.ShapeDtypeStruct((6, 3 * D), F32),
            jax.ShapeDtypeStruct((6, D), F32),
            jax.ShapeDtypeStruct((6, PIECES * R), F32),
            jax.ShapeDtypeStruct((32, R), F32),
        ),
        in_specs=[vmem] * 4 + [pl.BlockSpec(memory_space=pl.ANY)] * 4,
        out_specs=(vmem,) * 6,
        scratch_shapes=scratch,
        compiler_params=pltpu.CompilerParams(
            collective_id=1, has_side_effects=True, vmem_limit_bytes=63 * 1024 * 1024
        ),
        name="step",
    )(events, labels, counts, gain, w_qkv, w_out, w_piece, table)


def result_kernel(*refs):
    for src, dst in zip(refs[:5], refs[6:11]):
        dst[...] = src[...]
    refs[11][...] = refs[5][0, :6]


def results(rows, g_qkv, g_out, g_piece, g_table, gain):
    vmem = pl.BlockSpec(memory_space=pltpu.VMEM)
    like = [jax.ShapeDtypeStruct(a.shape, a.dtype) for a in (rows, g_qkv, g_out, g_piece, g_table)]
    return pl.pallas_call(
        result_kernel,
        out_shape=(*like, jax.ShapeDtypeStruct((6,), F32)),
        in_specs=[vmem] * 6,
        out_specs=(vmem,) * 6,
        name="results",
    )(rows, g_qkv, g_out, g_piece, g_table, gain)


def body(
    events,
    send_counts,
    patient_ids,
    codes,
    event_piece,
    censor_piece,
    norm_gain,
    w_qkv,
    w_out,
    w_piece,
    code_table,
):
    labels = jnp.concatenate([patient_ids[0], codes[0], event_piece[0], censor_piece[0]], 0)
    rows, gain, g_qkv, g_out, g_piece, g_table = step(
        events[0, 0], labels, send_counts[0], norm_gain[None], w_qkv, w_out, w_piece, code_table
    )
    rows, g_qkv, g_out, g_piece, g_table, g_gain = results(rows, g_qkv, g_out, g_piece, g_table, gain)
    return (rows[None, None], g_gain, g_qkv, g_out, g_piece, g_table)


def solution(mesh):
    split = P("win", "rep")
    return jax.shard_map(
        body,
        mesh=mesh,
        in_specs=(split,) * 6 + (P(),) * 5,
        out_specs=(split,) + (P(("win", "rep")),) * 5,
        check_vma=False,
    )
```

```python
import functools
import math

import jax
import jax.numpy as jnp
from jax import lax
from jax.experimental import pallas as pl
from jax.experimental.pallas import tpu as pltpu
from jax.sharding import PartitionSpec as P

HEADS = 12
EPSILON = 1e-05
MESH = pl.DeviceIdType.MESH

D = 768
PAIRS = 6
PIECES = 8
CODES = 4096
R = 128
ROWS = 512
EVENTS = 256
WIN = 32
SLOT = 16
LAB = 128
WIDE = D + LAB
BLOCK = 1024
LOG2E = math.log2(math.e)

F32 = jnp.float32
BF16 = jnp.bfloat16

NT = (((1,), (1,)), ((), ()))
TN = (((0,), (0,)), ((), ()))


def mm(a, b):
    return jnp.dot(a, b, preferred_element_type=F32)


def mm_nt(a, b):
    return lax.dot_general(a, b, NT, preferred_element_type=F32)


def mm_tn(a, b):
    return lax.dot_general(a, b, TN, preferred_element_type=F32)


def exchange_rows(src_ref, dst_ref, send_sem, recv_sem, me, low=1, high=WIN):
    @pl.loop(low, high)
    def _(k):
        peer = lax.rem(me + k, WIN)
        pltpu.make_async_remote_copy(
            src_ref=src_ref.at[peer],
            dst_ref=dst_ref.at[me],
            send_sem=send_sem.at[k],
            recv_sem=recv_sem.at[k],
            device_id={"win": peer},
            device_id_type=MESH,
        ).start()


def wait_rows(src_ref, dst_ref, send_sem, recv_sem, me):
    @pl.loop(1, WIN)
    def _(k):
        sender = lax.rem(me + WIN - k, WIN)
        pltpu.make_async_remote_copy(
            src_ref=src_ref.at[me],
            dst_ref=dst_ref.at[sender],
            send_sem=send_sem.at[k],
            recv_sem=recv_sem.at[k],
            device_id={"win": sender},
            device_id_type=MESH,
        ).wait()


def stack_halves(res):
    tiles = res.reshape(WIN, 3, 8, 256)
    both = jnp.concatenate([tiles[..., :128], tiles[..., 128:]], 2)
    return both.reshape(WIN, 48, 128).astype(BF16)


TODO = [(rb, head) for rb in range(2) for head in range(2)]


def span(rb):
    return slice(rb * 256, rb * 256 + 256)


def far(rb):
    return rb * 256 + 256


def lanes(index):
    return pl.ds(pl.multiple_of(index * 128, 128), 128)


ITEMS = (
    ("t", 128, 128, "zxy"),
    ("p", 48, 512, "yxz"),
    ("oa", 48, 256, "zxy"),
    ("ob", 48, 128, "xzy"),
    ("q0", 48, 128, "xzy"),
    ("k0", 48, 128, "zxy"),
    ("v0", 48, 128, "yxz"),
    ("q1", 48, 128, "xzy"),
    ("k1", 48, 128, "zxy"),
    ("v1", 48, 128, "yxz"),
    ("q2", 48, 128, "xzy"),
    ("k2", 48, 128, "zxy"),
    ("v2", 48, 128, "yxz"),
    ("g", 16, 128, "zxy"),
)
N_ITEMS = len(ITEMS)
INDEX = {item[0]: i for i, item in enumerate(ITEMS)}


def remote(src, dst, sems, index, where):
    return pltpu.make_async_remote_copy(
        src_ref=src,
        dst_ref=dst,
        send_sem=sems[0].at[index],
        recv_sem=sems[1].at[index],
        device_id=where,
        device_id_type=MESH,
    )


def step_kernel(
    ev_ref,
    lab_ref,
    cnt_ref,
    gain_ref,
    wqkv_any,
    wout_any,
    wpiece_any,
    table_any,
    rows_ref,
    gain_out,
    qkv_ref,
    out_ref,
    piece_ref,
    tab_ref,
    wqkv,
    wout,
    wpiece,
    table_ref,
    load_sem,
    hot_ref,
    packed,
    landed,
    rows_out,
    returned,
    there_send,
    there_recv,
    back_send,
    back_recv,
    sum_send,
    sum_recv,
    tab_send,
    tab_recv,
    src_t,
    src_p,
    src_oa,
    src_ob,
    src_qkv,
    src_g,
    perm,
    turned_p,
    tiles,
    normed,
    normed_t,
    qkv,
    prob,
    ctx,
    hidden,
    reps,
    reps_t,
    greps,
    own_row,
    fix,
    glow,
    ghid,
    gctx,
    dqkv,
    bias,
    labs,
    gnorm,
    *spare,
):
    bufs = [spare[6 * i : 6 * i + 6] for i in range(N_ITEMS)]
    sems = (sum_send, sum_recv)
    me = lax.axis_index("win")
    y = lax.axis_index("rep")
    core = lax.rem(me, 2)
    z_at = lax.rem(me // 2, 4)
    x_at = me // 8

    barrier = pltpu.get_barrier_semaphore()

    @pl.loop(1, WIN)
    def _(k):
        pl.semaphore_signal(
            barrier, inc=1, device_id={"win": lax.rem(me + k, WIN)}, device_id_type=MESH
        )

    @pl.loop(1, 4)
    def _(k):
        pl.semaphore_signal(
            barrier, inc=1, device_id={"rep": lax.rem(y + k, 4)}, device_id_type=MESH
        )

    loads = [
        pltpu.make_async_copy(src, dst, load_sem.at[i])
        for i, (src, dst) in enumerate(
            ((wqkv_any, wqkv), (wout_any, wout), (wpiece_any, wpiece), (table_any, table_ref))
        )
    ]
    for load in loads:
        load.start()

    counts = cnt_ref[...].astype(F32)
    row = lax.broadcasted_iota(jnp.int32, (ROWS, WIN), 0)
    owner = lax.broadcasted_iota(jnp.int32, (ROWS, WIN), 1)
    row_owner = row // SLOT
    mine = jnp.sum(jnp.where(owner == row_owner, counts, 0.0), 1, keepdims=True)
    start = jnp.sum(jnp.where(owner < row_owner, counts, 0.0), 1, keepdims=True)
    offset = (lax.broadcasted_iota(jnp.int32, (ROWS, 1), 0) % SLOT).astype(F32)
    place = lax.broadcasted_iota(jnp.int32, (ROWS, EVENTS), 1).astype(F32)
    wanted = jnp.where(offset < mine, start + offset, -1.0)
    hot = jnp.where(place == wanted, 1.0, 0.0).astype(BF16)
    hot_ref[...] = hot
    packed[:, :, :D] = mm(hot, ev_ref[...]).astype(BF16).reshape(WIN, SLOT, D)

    lab = lab_ref[...]
    high = lab[1:2] // 64
    rows = [lab[0:1], high, lab[1:2] - high * 64, lab[2:3], jnp.maximum(lab[2:3], lab[3:4])]
    rows.append(jnp.ones((1, EVENTS), jnp.int32))
    rows.append(jnp.zeros((2, EVENTS), jnp.int32))
    table = jnp.concatenate(rows, 0).astype(F32)
    table = jnp.concatenate([table, jnp.zeros((LAB - 8, EVENTS), F32)], 0).astype(BF16)
    packed[:, :, D:] = mm_nt(hot, table).astype(BF16).reshape(WIN, SLOT, LAB)

    pl.semaphore_wait(barrier, WIN - 1 + 3)
    exchange_rows(packed, landed, there_send, there_recv, me)
    landed[me] = packed[me]

    at = lax.broadcasted_iota(jnp.int32, (D, 1), 0)
    group, inner = at // 24, at % 24
    z_of, r_of = inner // 6, inner % 6
    y_of, x_of, core_of = group // 8, (group // 2) % 4, group % 2
    feature = ((x_of * 4 + z_of) * 2 + core_of) * 24 + y_of * 6 + r_of
    chosen = lax.broadcasted_iota(jnp.int32, (D, D), 1) == feature
    perm[...] = jnp.where(chosen, 1.0, 0.0).astype(BF16)

    wait_rows(packed, landed, there_send, there_recv, me)

    sources = {"t": src_t, "p": src_p, "oa": src_oa, "ob": src_ob, "g": src_g}
    for s in range(3):
        for part in range(3):
            sources["qkv"[part] + str(s)] = src_qkv.at[s, part]
    mine_at = {"x": x_at, "y": y, "z": z_at}

    def place_of(axis, k):
        return lax.rem(mine_at[axis] + k, 4)

    def device_of(axis, k):
        if axis == "x":
            return {"win": place_of("x", k) * 8 + z_at * 2 + core}
        if axis == "z":
            return {"win": x_at * 8 + place_of("z", k) * 2 + core}
        return {"rep": place_of("y", k)}

    def blocked(name):
        _, rows, width, _ = ITEMS[INDEX[name]]
        return sources[name].reshape(4, 4, 2, rows, width)

    def buf(name):
        return bufs[INDEX[name]]

    def core_copy(name):
        i = INDEX[name]
        return remote(
            blocked(name).at[:, :, 1 - core], buf(name)[0], sems, (i, 0), {"win": me + 1 - 2 * core}
        )

    def block_of(ref, order, first, second=None):
        if order in ("xzy", "yxz"):
            return ref.at[first] if second is None else ref.at[first, second]
        return ref.at[:, first] if second is None else ref.at[second, first]

    def ring_copy(name, step, k):
        i = INDEX[name]
        order = ITEMS[i][3]
        if step == 0:
            src = block_of(buf(name)[0], order, place_of(order[0], k))
        else:
            src = buf(name)[2].at[place_of(order[1], k)]
        return remote(
            src,
            buf(name)[1 + 2 * step].at[k - 1],
            sems,
            (i, 1 + 3 * step + k - 1),
            device_of(order[step], k),
        )

    def last_copy(name, k):
        axis = ITEMS[INDEX[name]][3][2]
        return remote(
            buf(name)[4].at[place_of(axis, k)],
            buf(name)[5].at[k - 1],
            sems,
            (INDEX[name], 7 + k - 1),
            device_of(axis, k),
        )

    def table_core(b):
        return remote(
            blocked("t").at[b, :, 1 - core],
            buf("t")[0].at[b],
            (tab_send, tab_recv),
            (b, 0),
            {"win": me + 1 - 2 * core},
        )

    def table_ring(b, k):
        return remote(
            buf("t")[0].at[b, place_of("z", k)],
            buf("t")[1].at[k - 1, b],
            (tab_send, tab_recv),
            (b, k),
            device_of("z", k),
        )

    def table_to_ring(b):
        table_core(b).wait()
        src, got = blocked("t"), buf("t")[0]
        for c in range(4):
            got[b, c] = (src[b, c, core].astype(F32) + got[b, c].astype(F32)).astype(BF16)
        for k in (2, 1, 3):
            table_ring(b, k).start()

    def begin(name):
        core_copy(name).start()

    def to_first_ring(name):
        core_copy(name).wait()
        src, got = blocked(name), buf(name)[0]
        for a in range(4):

            @pl.loop(0, 4)
            def _(b):
                got[a, b] = (src[a, b, core].astype(F32) + got[a, b].astype(F32)).astype(BF16)

        for k in (2, 1, 3):
            ring_copy(name, 0, k).start()

    def to_second_ring(name):
        order = ITEMS[INDEX[name]][3]
        if name == "t":

            @pl.loop(0, 4)
            def _(b):
                for k in (2, 1, 3):
                    table_ring(b, k).wait()
        else:
            for k in (2, 1, 3):
                ring_copy(name, 0, k).wait()
        mine, got, acc = buf(name)[0], buf(name)[1], buf(name)[2]

        @pl.loop(0, 4)
        def _(b):
            total = block_of(mine, order, place_of(order[0], 0), b)[...].astype(F32)
            for k in range(3):
                total += got[k, b].astype(F32)
            acc[b] = total.astype(BF16)

        for k in (2, 1, 3):
            ring_copy(name, 1, k).start()

    def to_last(name):
        _, rows, width, order = ITEMS[INDEX[name]]
        for k in (2, 1, 3):
            ring_copy(name, 1, k).wait()
        got = buf(name)[3]
        total = buf(name)[2][place_of(order[1], 0)].astype(F32)
        for k in range(3):
            total += got[k].astype(F32)
        low = buf(name)[4]
        if name == "t":
            low[...] = total.astype(BF16).reshape(4, 32, 128)
        elif name == "g":
            for yy in range(4):
                low[yy] = (pltpu.roll(total, 128 - 6 * yy, 1) if yy else total).astype(BF16)
        else:
            for half in range(2):
                for t in range(3):
                    at = t * 16 + half * 8
                    tiles[half, t * 8 : t * 8 + 8, :width] = total[at : at + 8]
            for yy in range(4):
                both = jnp.concatenate(
                    [tiles[0, 6 * yy : 6 * yy + 8, :width], tiles[1, 6 * yy : 6 * yy + 8, :width]], 0
                )
                low[yy] = both.astype(BF16)
        for k in (2, 1, 3):
            last_copy(name, k).start()

    def finish(name):
        _, rows, width, order = ITEMS[INDEX[name]]
        for k in (2, 1, 3):
            last_copy(name, k).wait()
        got = buf(name)[5]
        total = buf(name)[4][place_of(order[2], 0)].astype(F32)
        for k in range(3):
            total += got[k].astype(F32)
        total = total * (1.0 / math.sqrt(EVENTS * WIN * 4))
        if name == "t":
            tab_ref[...] = total
        elif name == "g":
            gain_out[...] = total[:8]
        else:
            for u in range(width // 128):
                if name == "p":
                    dst, at = piece_ref, u * 256
                elif name[0] == "o":
                    dst, at = out_ref, u * 256 if name == "oa" else 512
                else:
                    dst, at = qkv_ref, "qkv".index(name[0]) * D + int(name[1]) * 256
                us = slice(u * 128, u * 128 + 128)
                dst[:, at : at + 128] = total[:6, us]
                dst[:, at + 128 : at + 256] = total[8:14, us]

    gain = gain_ref[...]
    lab = landed[:, :, D:].reshape(ROWS, LAB).astype(F32)
    valid = lab[:, 5:6] > 0.5
    patient = jnp.where(valid, lab[:, 0:1], -1.0)
    labs[0] = jnp.broadcast_to(lab[:, 1:2] * 64.0 + lab[:, 2:3], (ROWS, 128))
    labs[1] = jnp.broadcast_to(jnp.where(valid, lab[:, 3:4], -1.0), (ROWS, 128))
    labs[2] = jnp.broadcast_to(jnp.where(valid, lab[:, 4:5], -1.0), (ROWS, 128))

    lab_t = lab.T
    patient_row = jnp.where(lab_t[5:6] > 0.5, lab_t[0:1], -1.0)
    row = lax.broadcasted_iota(jnp.int32, (ROWS, ROWS), 0)
    col = lax.broadcasted_iota(jnp.int32, (ROWS, ROWS), 1)
    allowed = ((patient == patient_row) & (col <= row)) | (col == row)
    bias[...] = jnp.where(allowed, 0.0, -1e30)

    x = landed[:, :, :D].reshape(ROWS, D).astype(F32)
    inv_rms = lax.rsqrt(jnp.mean(x * x, -1, keepdims=True) + EPSILON)
    normed[...] = (x * inv_rms * gain).astype(BF16)

    loads[0].wait()

    @pl.loop(0, 9)
    def _(j):
        cols = pl.ds(pl.multiple_of(j * 256, 256), 256)
        res = mm(normed[...], wqkv[:, cols])
        scale = jnp.where(j < 3, 0.125, 1.0)
        res = (res * scale).astype(BF16)
        qkv[2 * j] = res[:, :128]
        qkv[2 * j + 1] = res[:, 128:]

    low_lanes = lax.broadcasted_iota(jnp.int32, (1, 128), 1) < 64

    def head_part(value, head):
        zero = jnp.zeros((), value.dtype)
        return jnp.where(low_lanes, value, zero) if head == 0 else jnp.where(low_lanes, zero, value)

    @pl.loop(0, PAIRS, unroll=2)
    def _(p):
        q = qkv[p]
        k = qkv[PAIRS + p]
        v = qkv[2 * PAIRS + p]
        s = [mm_nt(head_part(q[span(rb)], head), k[: far(rb)]) + bias[span(rb), : far(rb)] for rb, head in TODO]
        top = [jnp.max(a, -1, keepdims=True) for a in s]
        w = [jnp.exp(a - m) for a, m in zip(s, top)]
        inv = [1.0 / jnp.sum(a, -1, keepdims=True) for a in w]
        pr = [(a * i).astype(BF16) for a, i in zip(w, inv)]
        for (rb, head), a in zip(TODO, pr):
            prob[p, head, span(rb), : far(rb)] = a
        got = [mm(a, v[: far(rb)]) for (rb, head), a in zip(TODO, pr)]
        for rb in range(2):
            ctx[span(rb), lanes(p)] = jnp.where(low_lanes, got[2 * rb], got[2 * rb + 1]).astype(BF16)

    loads[1].wait()

    @pl.loop(0, 3)
    def _(j):
        cols = pl.ds(pl.multiple_of(j * 256, 256), 256)
        res = mm(ctx[...], wout[:, cols])
        hidden[:, cols] = (landed[:, :, cols].reshape(ROWS, 256).astype(F32) + res).astype(BF16)

    loads[2].wait()

    @pl.loop(0, 4)
    def _(j):
        cols = pl.ds(pl.multiple_of(j * 256, 256), 256)
        res = mm(hidden[...], wpiece[:, cols])
        for i in range(2):
            part = res[:, i * 128 : i * 128 + 128]
            reps[2 * j + i] = part.astype(BF16)
            reps_t[2 * j + i] = part.T.astype(BF16)

    loads[3].wait()

    log_codes = math.log2(CODES)
    times = BLOCK // 128
    code, event, end = labs[0], labs[1], labs[2]
    own_code = jnp.where(event >= 0, code, -1.0)

    def widen(tile):
        return jnp.concatenate([tile] * times, 1)

    def block_ids(b):
        return (b * BLOCK + lax.broadcasted_iota(jnp.int32, (1, BLOCK), 1)).astype(F32)

    def block_at(b):
        return pl.ds(pl.multiple_of(b * BLOCK, BLOCK), BLOCK)

    own_row[...] = jnp.zeros_like(own_row)

    @pl.loop(0, CODES // BLOCK)
    def _(b):
        hot = jnp.where(widen(own_code) == block_ids(b), 1.0, 0.0).astype(BF16)
        own_row[...] += mm(hot, table_ref[block_at(b), :])

    for p in range(PIECES):
        at_code = jnp.sum(reps[p].astype(F32) * own_row[...], -1, keepdims=True)
        value = jnp.exp2(at_code * LOG2E - log_codes) - 1.0
        fix[p] = jnp.where(event == p, value, 0.0)

    greps[...] = jnp.zeros_like(greps)

    @pl.loop(0, CODES // BLOCK)
    def _(b):
        tab = table_ref[block_at(b), :]
        ids = block_ids(b)

        def weights(p, logits):
            live = widen(jnp.where(end >= p, -log_codes, -1e30))
            e = jnp.exp2(logits * LOG2E + live)
            act = widen(jnp.where(event <= p, own_code, -1.0))
            return jnp.where(act == ids, widen(fix[p]), e).astype(BF16)

        logits = mm_nt(reps[0], tab)
        total = jnp.zeros((R, BLOCK), F32)
        for p in range(PIECES):
            after = mm_nt(reps[p + 1], tab) if p + 1 < PIECES else None
            g = weights(p, logits)
            greps[p] += mm(g, tab)
            total = total + mm(reps_t[p], g)
            logits = after
        turned = total.T.astype(BF16).reshape(BLOCK // 128, 128, 128)
        src_t[pl.ds(b * (BLOCK // 128), BLOCK // 128)] = turned
        table_core(b).start()

        @pl.when(b > 0)
        def _():
            table_to_ring(b - 1)

    table_to_ring(3)

    for p in range(PIECES):
        glow[:, p * 128 : p * 128 + 128] = greps[p].astype(BF16)

    turned_p[...] = mm_nt(perm[...], hidden[...]).astype(BF16)
    for j in range(4):
        cols = slice(j * 256, j * 256 + 256)
        src_p[:, :, j * 128 : j * 128 + 128] = stack_halves(mm(turned_p[...], glow[:, cols]))
    begin("p")

    for j in range(3):
        cols = slice(j * 256, j * 256 + 256)
        ghid[:, cols] = mm_nt(glow[...], wpiece[cols, :]).astype(BF16)

    ctx_t = ctx[...].T
    for j in range(3):
        cols = slice(j * 256, j * 256 + 256)
        res = stack_halves(mm(ctx_t, ghid[:, cols]))
        if j < 2:
            src_oa[:, :, j * 128 : j * 128 + 128] = res
        else:
            src_ob[...] = res
    begin("oa")
    begin("ob")
    to_first_ring("p")

    for j in range(3):
        cols = slice(j * 256, j * 256 + 256)
        gctx[:, cols] = mm_nt(ghid[...], wout[cols, :]).astype(BF16)
    to_first_ring("oa")
    to_first_ring("ob")
    normed_t[...] = normed[...].T
    turned_p[...] = mm_nt(perm[...], normed[...]).astype(BF16)
    to_second_ring("t")

    def backward_pair(p):
        q = qkv[p]
        k = qkv[PAIRS + p]
        v = qkv[2 * PAIRS + p]
        g = gctx[:, lanes(p)]
        gh = [head_part(g[span(rb)], head) for rb, head in TODO]
        low = [prob[p, head, span(rb), : far(rb)] for rb, head in TODO]
        dp = [mm_nt(a, v[: far(rb)]) for (rb, head), a in zip(TODO, gh)]
        inner = [jnp.sum(a * b.astype(F32), -1, keepdims=True) for a, b in zip(dp, low)]
        ds = [(b.astype(F32) * (a - i)).astype(BF16) for a, b, i in zip(dp, low, inner)]
        cat = lambda a, i: jnp.concatenate([a[i], a[i + 1]], 0)
        dv = [mm_tn(cat(low, i), cat(gh, i)) for i in (0, 2)]
        dq = [mm(a, k[: far(rb)]) for (rb, head), a in zip(TODO, ds)]
        qh = [head_part(q[span(rb)], head) for rb, head in TODO]
        dk = [mm_tn(cat(ds, i), cat(qh, i)) for i in (0, 2)]
        for rb in range(2):
            both = jnp.where(low_lanes, dq[2 * rb], dq[2 * rb + 1]) * 0.125
            dqkv[span(rb), lanes(p)] = both.astype(BF16)
        for at, parts in ((PAIRS, dk), (2 * PAIRS, dv)):
            wide = parts[1]
            dqkv[:256, lanes(at + p)] = (wide[:256] + parts[0]).astype(BF16)
            dqkv[256:, lanes(at + p)] = wide[256:].astype(BF16)

    def backward_step(s):
        pl.loop(2 * s, 2 * s + 2, unroll=2)(backward_pair)

    def qkv_step(s):
        for part in (2, 0, 1):
            cols = slice(part * D + s * 256, part * D + s * 256 + 256)
            left = turned_p if part == 2 else normed_t
            src_qkv[s, part] = stack_halves(mm(left[...], dqkv[:, cols]))
            begin("qkv"[part] + str(s))

    def each(stage, s):
        for part in "vqk":
            stage(part + str(s))

    backward_step(0)
    qkv_step(0)
    to_last("t")
    backward_step(1)
    each(to_first_ring, 0)
    qkv_step(1)
    backward_step(2)
    each(to_first_ring, 1)
    qkv_step(2)
    to_second_ring("p")
    to_second_ring("oa")
    to_second_ring("ob")

    for j in range(3):
        cols = slice(j * 256, j * 256 + 256)
        gnorm[:, cols] = mm_nt(dqkv[...], wqkv[cols, :])

    x = landed[:, :, :D].reshape(ROWS, D).astype(F32)
    inv_rms = lax.rsqrt(jnp.mean(x * x, -1, keepdims=True) + EPSILON)
    x_hat = x * inv_rms
    gn = gnorm[...]
    ggain = jnp.sum(gn * x_hat, 0, keepdims=True)
    feature = lax.broadcasted_iota(jnp.int32, (ROWS, D), 1)
    block = lax.broadcasted_iota(jnp.int32, (ROWS, D), 0) // SLOT
    spread = jnp.where(feature // 24 == block, ggain, 0.0).astype(BF16)
    pick = lax.broadcasted_iota(jnp.int32, (D, 128), 0) % 24
    pick = jnp.where(pick == lax.broadcasted_iota(jnp.int32, (D, 128), 1), 1.0, 0.0).astype(BF16)
    src_g[...] = mm(spread, pick).astype(BF16).reshape(WIN, SLOT, 128)
    begin("g")
    each(to_first_ring, 2)

    gh = gn * gain
    gx = inv_rms * (gh - x_hat * jnp.mean(gh * x_hat, -1, keepdims=True))
    gb = (gx + ghid[...].astype(F32)).astype(BF16)
    rows_out[...] = gb.reshape(WIN, SLOT, D)
    to_first_ring("g")
    exchange_rows(rows_out, returned, back_send, back_recv, me, 1, 12)
    each(to_second_ring, 0)
    exchange_rows(rows_out, returned, back_send, back_recv, me, 12, 22)
    to_last("p")
    to_last("oa")
    to_last("ob")
    each(to_second_ring, 1)
    exchange_rows(rows_out, returned, back_send, back_recv, me, 22, WIN)
    returned[me] = rows_out[me]
    to_second_ring("g")
    each(to_last, 0)
    each(to_second_ring, 2)
    each(to_last, 1)
    to_last("g")
    for name in ("t", "p", "oa", "ob"):
        finish(name)
    each(finish, 0)
    each(to_last, 2)
    each(finish, 1)
    wait_rows(rows_out, returned, back_send, back_recv, me)
    rows_ref[...] = mm_tn(hot_ref[...], returned[...].reshape(ROWS, D)).astype(BF16)
    finish("g")
    each(finish, 2)


def step(events, labels, counts, gain, w_qkv, w_out, w_piece, table):
    vmem = pl.BlockSpec(memory_space=pltpu.VMEM)
    scratch = [
        pltpu.VMEM((D, 3 * D), BF16),
        pltpu.VMEM((D, D), BF16),
        pltpu.VMEM((D, PIECES * R), BF16),
        pltpu.VMEM((CODES, R), BF16),
        pltpu.SemaphoreType.DMA((4,)),
        pltpu.VMEM((ROWS, EVENTS), BF16),
        pltpu.VMEM((WIN, SLOT, WIDE), BF16),
        pltpu.VMEM((WIN, SLOT, WIDE), BF16),
        pltpu.VMEM((WIN, SLOT, D), BF16),
        pltpu.VMEM((WIN, SLOT, D), BF16),
        pltpu.SemaphoreType.DMA((WIN,)),
        pltpu.SemaphoreType.DMA((WIN,)),
        pltpu.SemaphoreType.DMA((WIN,)),
        pltpu.SemaphoreType.DMA((WIN,)),
        pltpu.SemaphoreType.DMA((N_ITEMS, 10)),
        pltpu.SemaphoreType.DMA((N_ITEMS, 10)),
        pltpu.SemaphoreType.DMA((4, 4)),
        pltpu.SemaphoreType.DMA((4, 4)),
        pltpu.VMEM((WIN, 128, 128), BF16),
        pltpu.VMEM((WIN, 48, 512), BF16),
        pltpu.VMEM((WIN, 48, 256), BF16),
        pltpu.VMEM((WIN, 48, 128), BF16),
        pltpu.VMEM((3, 3, WIN, 48, 128), BF16),
        pltpu.VMEM((WIN, SLOT, 128), BF16),
        pltpu.VMEM((D, D), BF16),
        pltpu.VMEM((D, ROWS), BF16),
        pltpu.VMEM((2, 32, 512), F32),
        pltpu.VMEM((ROWS, D), BF16),
        pltpu.VMEM((D, ROWS), BF16),
        pltpu.VMEM((18, ROWS, 128), BF16),
        pltpu.VMEM((PAIRS, 2, ROWS, ROWS), BF16),
        pltpu.VMEM((ROWS, D), BF16),
        pltpu.VMEM((ROWS, D), BF16),
        pltpu.VMEM((PIECES, ROWS, R), BF16),
        pltpu.VMEM((PIECES, R, ROWS), BF16),
        pltpu.VMEM((PIECES, ROWS, R), F32),
        pltpu.VMEM((ROWS, R), F32),
        pltpu.VMEM((PIECES, ROWS, 128), F32),
        pltpu.VMEM((ROWS, PIECES * R), BF16),
        pltpu.VMEM((ROWS, D), BF16),
        pltpu.VMEM((ROWS, D), BF16),
        pltpu.VMEM((ROWS, 3 * D), BF16),
        pltpu.VMEM((ROWS, ROWS), F32),
        pltpu.VMEM((3, ROWS, 128), F32),
        pltpu.VMEM((ROWS, D), F32),
    ]
    for name, rows, width, order in ITEMS:
        last = 32 if name == "t" else 16
        scratch += [
            pltpu.VMEM((4, 4, rows, width), BF16),
            pltpu.VMEM((3, 4, rows, width), BF16),
            pltpu.VMEM((4, rows, width), BF16),
            pltpu.VMEM((3, rows, width), BF16),
            pltpu.VMEM((4, last, width), BF16),
            pltpu.VMEM((3, last, width), BF16),
        ]
    return pl.pallas_call(
        step_kernel,
        out_shape=(
            jax.ShapeDtypeStruct((EVENTS, D), BF16),
            jax.ShapeDtypeStruct((8, 128), F32),
            jax.ShapeDtypeStruct((6, 3 * D), F32),
            jax.ShapeDtypeStruct((6, D), F32),
            jax.ShapeDtypeStruct((6, PIECES * R), F32),
            jax.ShapeDtypeStruct((32, R), F32),
        ),
        in_specs=[vmem] * 4 + [pl.BlockSpec(memory_space=pl.ANY)] * 4,
        out_specs=(vmem,) * 6,
        scratch_shapes=scratch,
        compiler_params=pltpu.CompilerParams(
            collective_id=1, has_side_effects=True, vmem_limit_bytes=63 * 1024 * 1024
        ),
        name="step",
    )(events, labels, counts, gain, w_qkv, w_out, w_piece, table)


def result_kernel(*refs):
    for src, dst in zip(refs[:5], refs[6:11]):
        dst[...] = src[...]
    refs[11][...] = refs[5][0, :6]


def results(rows, g_qkv, g_out, g_piece, g_table, gain):
    vmem = pl.BlockSpec(memory_space=pltpu.VMEM)
    like = [jax.ShapeDtypeStruct(a.shape, a.dtype) for a in (rows, g_qkv, g_out, g_piece, g_table)]
    return pl.pallas_call(
        result_kernel,
        out_shape=(*like, jax.ShapeDtypeStruct((6,), F32)),
        in_specs=[vmem] * 6,
        out_specs=(vmem,) * 6,
        name="results",
    )(rows, g_qkv, g_out, g_piece, g_table, gain)


def body(
    events,
    send_counts,
    patient_ids,
    codes,
    event_piece,
    censor_piece,
    norm_gain,
    w_qkv,
    w_out,
    w_piece,
    code_table,
):
    labels = jnp.concatenate([patient_ids[0], codes[0], event_piece[0], censor_piece[0]], 0)
    rows, gain, g_qkv, g_out, g_piece, g_table = step(
        events[0, 0], labels, send_counts[0], norm_gain[None], w_qkv, w_out, w_piece, code_table
    )
    rows, g_qkv, g_out, g_piece, g_table, g_gain = results(rows, g_qkv, g_out, g_piece, g_table, gain)
    return (rows[None, None], g_gain, g_qkv, g_out, g_piece, g_table)


def solution(mesh):
    split = P("win", "rep")
    return jax.shard_map(
        body,
        mesh=mesh,
        in_specs=(split,) * 6 + (P(),) * 5,
        out_specs=(split,) + (P(("win", "rep")),) * 5,
        check_vma=False,
    )
```

```python
import functools
import math

import jax
import jax.numpy as jnp
from jax import lax
from jax.experimental import pallas as pl
from jax.experimental.pallas import tpu as pltpu
from jax.sharding import PartitionSpec as P

HEADS = 12
EPSILON = 1e-05
MESH = pl.DeviceIdType.MESH

D = 768
PAIRS = 6
PIECES = 8
CODES = 4096
R = 128
ROWS = 512
EVENTS = 256
WIN = 32
SLOT = 16
LAB = 128
WIDE = D + LAB
BLOCK = 1024
LOG2E = math.log2(math.e)

F32 = jnp.float32
BF16 = jnp.bfloat16

NT = (((1,), (1,)), ((), ()))
TN = (((0,), (0,)), ((), ()))


def mm(a, b):
    return jnp.dot(a, b, preferred_element_type=F32)


def mm_nt(a, b):
    return lax.dot_general(a, b, NT, preferred_element_type=F32)


def mm_tn(a, b):
    return lax.dot_general(a, b, TN, preferred_element_type=F32)


def exchange_rows(src_ref, dst_ref, send_sem, recv_sem, me, low=1, high=WIN):
    @pl.loop(low, high)
    def _(k):
        peer = lax.rem(me + k, WIN)
        pltpu.make_async_remote_copy(
            src_ref=src_ref.at[peer],
            dst_ref=dst_ref.at[me],
            send_sem=send_sem.at[k],
            recv_sem=recv_sem.at[k],
            device_id={"win": peer},
            device_id_type=MESH,
        ).start()


def wait_rows(src_ref, dst_ref, send_sem, recv_sem, me):
    @pl.loop(1, WIN)
    def _(k):
        sender = lax.rem(me + WIN - k, WIN)
        pltpu.make_async_remote_copy(
            src_ref=src_ref.at[me],
            dst_ref=dst_ref.at[sender],
            send_sem=send_sem.at[k],
            recv_sem=recv_sem.at[k],
            device_id={"win": sender},
            device_id_type=MESH,
        ).wait()


def stack_halves(res):
    tiles = res.reshape(WIN, 3, 8, 256)
    both = jnp.concatenate([tiles[..., :128], tiles[..., 128:]], 2)
    return both.reshape(WIN, 48, 128).astype(BF16)


TODO = [(rb, head) for rb in range(2) for head in range(2)]


def span(rb):
    return slice(rb * 256, rb * 256 + 256)


def far(rb):
    return rb * 256 + 256


def lanes(index):
    return pl.ds(pl.multiple_of(index * 128, 128), 128)


ITEMS = (
    ("t", 128, 128, "zxy"),
    ("p", 48, 512, "yxz"),
    ("o", 48, 384, "zxy"),
    ("a0", 48, 256, "xzy"),
    ("v0", 48, 128, "yxz"),
    ("a1", 48, 256, "zxy"),
    ("v1", 48, 128, "yxz"),
    ("a2", 48, 256, "xzy"),
    ("v2", 48, 128, "yxz"),
    ("g", 16, 128, "zxy"),
)
N_ITEMS = len(ITEMS)
INDEX = {item[0]: i for i, item in enumerate(ITEMS)}


def remote(src, dst, sems, index, where):
    return pltpu.make_async_remote_copy(
        src_ref=src,
        dst_ref=dst,
        send_sem=sems[0].at[index],
        recv_sem=sems[1].at[index],
        device_id=where,
        device_id_type=MESH,
    )


def step_kernel(
    ev_ref,
    lab_ref,
    cnt_ref,
    gain_ref,
    wqkv_any,
    wout_any,
    wpiece_any,
    table_any,
    rows_ref,
    gain_out,
    qkv_ref,
    out_ref,
    piece_ref,
    tab_ref,
    wqkv,
    wout,
    wpiece,
    table_ref,
    load_sem,
    hot_ref,
    packed,
    landed,
    rows_out,
    returned,
    there_send,
    there_recv,
    back_send,
    back_recv,
    sum_send,
    sum_recv,
    tab_send,
    tab_recv,
    src_t,
    src_p,
    src_o,
    src_a,
    src_v,
    src_g,
    perm,
    turned_p,
    tiles,
    normed,
    normed_t,
    qkv,
    prob,
    ctx,
    hidden,
    reps,
    reps_t,
    greps,
    own_row,
    fix,
    glow,
    ghid,
    gctx,
    dqkv,
    bias,
    labs,
    gnorm,
    *spare,
):
    bufs = [spare[6 * i : 6 * i + 6] for i in range(N_ITEMS)]
    sems = (sum_send, sum_recv)
    me = lax.axis_index("win")
    y = lax.axis_index("rep")
    core = lax.rem(me, 2)
    z_at = lax.rem(me // 2, 4)
    x_at = me // 8

    barrier = pltpu.get_barrier_semaphore()

    @pl.loop(1, WIN)
    def _(k):
        pl.semaphore_signal(
            barrier, inc=1, device_id={"win": lax.rem(me + k, WIN)}, device_id_type=MESH
        )

    @pl.loop(1, 4)
    def _(k):
        pl.semaphore_signal(
            barrier, inc=1, device_id={"rep": lax.rem(y + k, 4)}, device_id_type=MESH
        )

    loads = [
        pltpu.make_async_copy(src, dst, load_sem.at[i])
        for i, (src, dst) in enumerate(
            ((wqkv_any, wqkv), (wout_any, wout), (wpiece_any, wpiece), (table_any, table_ref))
        )
    ]
    for load in loads:
        load.start()

    counts = cnt_ref[...].astype(F32)
    row = lax.broadcasted_iota(jnp.int32, (ROWS, WIN), 0)
    owner = lax.broadcasted_iota(jnp.int32, (ROWS, WIN), 1)
    row_owner = row // SLOT
    mine = jnp.sum(jnp.where(owner == row_owner, counts, 0.0), 1, keepdims=True)
    start = jnp.sum(jnp.where(owner < row_owner, counts, 0.0), 1, keepdims=True)
    offset = (lax.broadcasted_iota(jnp.int32, (ROWS, 1), 0) % SLOT).astype(F32)
    place = lax.broadcasted_iota(jnp.int32, (ROWS, EVENTS), 1).astype(F32)
    wanted = jnp.where(offset < mine, start + offset, -1.0)
    hot = jnp.where(place == wanted, 1.0, 0.0).astype(BF16)
    hot_ref[...] = hot
    packed[:, :, :D] = mm(hot, ev_ref[...]).astype(BF16).reshape(WIN, SLOT, D)

    lab = lab_ref[...]
    high = lab[1:2] // 64
    rows = [lab[0:1], high, lab[1:2] - high * 64, lab[2:3], jnp.maximum(lab[2:3], lab[3:4])]
    rows.append(jnp.ones((1, EVENTS), jnp.int32))
    rows.append(jnp.zeros((2, EVENTS), jnp.int32))
    table = jnp.concatenate(rows, 0).astype(F32)
    table = jnp.concatenate([table, jnp.zeros((LAB - 8, EVENTS), F32)], 0).astype(BF16)
    packed[:, :, D:] = mm_nt(hot, table).astype(BF16).reshape(WIN, SLOT, LAB)

    pl.semaphore_wait(barrier, WIN - 1 + 3)
    exchange_rows(packed, landed, there_send, there_recv, me)
    landed[me] = packed[me]

    at = lax.broadcasted_iota(jnp.int32, (D, 1), 0)
    group, inner = at // 24, at % 24
    z_of, r_of = inner // 6, inner % 6
    y_of, x_of, core_of = group // 8, (group // 2) % 4, group % 2
    feature = ((x_of * 4 + z_of) * 2 + core_of) * 24 + y_of * 6 + r_of
    chosen = lax.broadcasted_iota(jnp.int32, (D, D), 1) == feature
    perm[...] = jnp.where(chosen, 1.0, 0.0).astype(BF16)

    wait_rows(packed, landed, there_send, there_recv, me)

    sources = {"t": src_t, "p": src_p, "o": src_o, "g": src_g}
    for s in range(3):
        sources["a%d" % s] = src_a.at[s]
        sources["v%d" % s] = src_v.at[s]
    mine_at = {"x": x_at, "y": y, "z": z_at}

    def place_of(axis, k):
        return lax.rem(mine_at[axis] + k, 4)

    def device_of(axis, k):
        if axis == "x":
            return {"win": place_of("x", k) * 8 + z_at * 2 + core}
        if axis == "z":
            return {"win": x_at * 8 + place_of("z", k) * 2 + core}
        return {"rep": place_of("y", k)}

    def blocked(name):
        _, rows, width, _ = ITEMS[INDEX[name]]
        return sources[name].reshape(4, 4, 2, rows, width)

    def buf(name):
        return bufs[INDEX[name]]

    def core_copy(name):
        i = INDEX[name]
        return remote(
            blocked(name).at[:, :, 1 - core], buf(name)[0], sems, (i, 0), {"win": me + 1 - 2 * core}
        )

    def block_of(ref, order, first, second=None):
        if order in ("xzy", "yxz"):
            return ref.at[first] if second is None else ref.at[first, second]
        return ref.at[:, first] if second is None else ref.at[second, first]

    def ring_copy(name, step, k):
        i = INDEX[name]
        order = ITEMS[i][3]
        if step == 0:
            src = block_of(buf(name)[0], order, place_of(order[0], k))
        else:
            src = buf(name)[2].at[place_of(order[1], k)]
        return remote(
            src,
            buf(name)[1 + 2 * step].at[k - 1],
            sems,
            (i, 1 + 3 * step + k - 1),
            device_of(order[step], k),
        )

    def last_copy(name, k):
        axis = ITEMS[INDEX[name]][3][2]
        return remote(
            buf(name)[4].at[place_of(axis, k)],
            buf(name)[5].at[k - 1],
            sems,
            (INDEX[name], 7 + k - 1),
            device_of(axis, k),
        )

    def table_core(b):
        return remote(
            blocked("t").at[b, :, 1 - core],
            buf("t")[0].at[b],
            (tab_send, tab_recv),
            (b, 0),
            {"win": me + 1 - 2 * core},
        )

    def table_ring(b, k):
        return remote(
            buf("t")[0].at[b, place_of("z", k)],
            buf("t")[1].at[k - 1, b],
            (tab_send, tab_recv),
            (b, k),
            device_of("z", k),
        )

    def table_to_ring(b):
        table_core(b).wait()
        src, got = blocked("t"), buf("t")[0]
        for c in range(4):
            got[b, c] = (src[b, c, core].astype(F32) + got[b, c].astype(F32)).astype(BF16)
        for k in (2, 1, 3):
            table_ring(b, k).start()

    def begin(name):
        core_copy(name).start()

    def to_first_ring(name):
        core_copy(name).wait()
        src, got = blocked(name), buf(name)[0]
        for a in range(4):

            @pl.loop(0, 4)
            def _(b):
                got[a, b] = (src[a, b, core].astype(F32) + got[a, b].astype(F32)).astype(BF16)

        for k in (2, 1, 3):
            ring_copy(name, 0, k).start()

    def to_second_ring(name):
        order = ITEMS[INDEX[name]][3]
        if name == "t":

            @pl.loop(0, 4)
            def _(b):
                for k in (2, 1, 3):
                    table_ring(b, k).wait()
        else:
            for k in (2, 1, 3):
                ring_copy(name, 0, k).wait()
        mine, got, acc = buf(name)[0], buf(name)[1], buf(name)[2]

        @pl.loop(0, 4)
        def _(b):
            total = block_of(mine, order, place_of(order[0], 0), b)[...].astype(F32)
            for k in range(3):
                total += got[k, b].astype(F32)
            acc[b] = total.astype(BF16)

        for k in (2, 1, 3):
            ring_copy(name, 1, k).start()

    def to_last(name):
        _, rows, width, order = ITEMS[INDEX[name]]
        for k in (2, 1, 3):
            ring_copy(name, 1, k).wait()
        got = buf(name)[3]
        total = buf(name)[2][place_of(order[1], 0)].astype(F32)
        for k in range(3):
            total += got[k].astype(F32)
        low = buf(name)[4]
        if name == "t":
            low[...] = total.astype(BF16).reshape(4, 32, 128)
        elif name == "g":
            for yy in range(4):
                low[yy] = (pltpu.roll(total, 128 - 6 * yy, 1) if yy else total).astype(BF16)
        else:
            for half in range(2):
                for t in range(3):
                    at = t * 16 + half * 8
                    tiles[half, t * 8 : t * 8 + 8, :width] = total[at : at + 8]
            for yy in range(4):
                both = jnp.concatenate(
                    [tiles[0, 6 * yy : 6 * yy + 8, :width], tiles[1, 6 * yy : 6 * yy + 8, :width]], 0
                )
                low[yy] = both.astype(BF16)
        for k in (2, 1, 3):
            last_copy(name, k).start()

    def finish(name):
        _, rows, width, order = ITEMS[INDEX[name]]
        for k in (2, 1, 3):
            last_copy(name, k).wait()
        got = buf(name)[5]
        total = buf(name)[4][place_of(order[2], 0)].astype(F32)
        for k in range(3):
            total += got[k].astype(F32)
        total = total * (1.0 / math.sqrt(EVENTS * WIN * 4))
        if name == "t":
            tab_ref[...] = total
        elif name == "g":
            gain_out[...] = total[:8]
        else:
            for u in range(width // 128):
                if name == "p":
                    dst, at = piece_ref, u * 256
                elif name == "o":
                    dst, at = out_ref, u * 256
                else:
                    part = u if name[0] == "a" else 2
                    dst, at = qkv_ref, part * D + int(name[1]) * 256
                us = slice(u * 128, u * 128 + 128)
                dst[:, at : at + 128] = total[:6, us]
                dst[:, at + 128 : at + 256] = total[8:14, us]

    gain = gain_ref[...]
    lab = landed[:, :, D:].reshape(ROWS, LAB).astype(F32)
    valid = lab[:, 5:6] > 0.5
    patient = jnp.where(valid, lab[:, 0:1], -1.0)
    labs[0] = jnp.broadcast_to(lab[:, 1:2] * 64.0 + lab[:, 2:3], (ROWS, 128))
    labs[1] = jnp.broadcast_to(jnp.where(valid, lab[:, 3:4], -1.0), (ROWS, 128))
    labs[2] = jnp.broadcast_to(jnp.where(valid, lab[:, 4:5], -1.0), (ROWS, 128))

    lab_t = lab.T
    patient_row = jnp.where(lab_t[5:6] > 0.5, lab_t[0:1], -1.0)
    row = lax.broadcasted_iota(jnp.int32, (ROWS, ROWS), 0)
    col = lax.broadcasted_iota(jnp.int32, (ROWS, ROWS), 1)
    allowed = ((patient == patient_row) & (col <= row)) | (col == row)
    bias[...] = jnp.where(allowed, 0.0, -1e30)

    x = landed[:, :, :D].reshape(ROWS, D).astype(F32)
    inv_rms = lax.rsqrt(jnp.mean(x * x, -1, keepdims=True) + EPSILON)
    normed[...] = (x * inv_rms * gain).astype(BF16)

    loads[0].wait()

    @pl.loop(0, 9)
    def _(j):
        cols = pl.ds(pl.multiple_of(j * 256, 256), 256)
        res = mm(normed[...], wqkv[:, cols])
        scale = jnp.where(j < 3, 0.125, 1.0)
        res = (res * scale).astype(BF16)
        qkv[2 * j] = res[:, :128]
        qkv[2 * j + 1] = res[:, 128:]

    low_lanes = lax.broadcasted_iota(jnp.int32, (1, 128), 1) < 64

    def head_part(value, head):
        zero = jnp.zeros((), value.dtype)
        return jnp.where(low_lanes, value, zero) if head == 0 else jnp.where(low_lanes, zero, value)

    @pl.loop(0, PAIRS, unroll=2)
    def _(p):
        q = qkv[p]
        k = qkv[PAIRS + p]
        v = qkv[2 * PAIRS + p]
        s = [mm_nt(head_part(q[span(rb)], head), k[: far(rb)]) + bias[span(rb), : far(rb)] for rb, head in TODO]
        top = [jnp.max(a, -1, keepdims=True) for a in s]
        w = [jnp.exp(a - m) for a, m in zip(s, top)]
        inv = [1.0 / jnp.sum(a, -1, keepdims=True) for a in w]
        pr = [(a * i).astype(BF16) for a, i in zip(w, inv)]
        for (rb, head), a in zip(TODO, pr):
            prob[p, head, span(rb), : far(rb)] = a
        got = [mm(a, v[: far(rb)]) for (rb, head), a in zip(TODO, pr)]
        for rb in range(2):
            ctx[span(rb), lanes(p)] = jnp.where(low_lanes, got[2 * rb], got[2 * rb + 1]).astype(BF16)

    loads[1].wait()

    @pl.loop(0, 3)
    def _(j):
        cols = pl.ds(pl.multiple_of(j * 256, 256), 256)
        res = mm(ctx[...], wout[:, cols])
        hidden[:, cols] = (landed[:, :, cols].reshape(ROWS, 256).astype(F32) + res).astype(BF16)

    loads[2].wait()

    @pl.loop(0, 4)
    def _(j):
        cols = pl.ds(pl.multiple_of(j * 256, 256), 256)
        res = mm(hidden[...], wpiece[:, cols])
        for i in range(2):
            part = res[:, i * 128 : i * 128 + 128]
            reps[2 * j + i] = part.astype(BF16)
            reps_t[2 * j + i] = part.T.astype(BF16)

    loads[3].wait()

    log_codes = math.log2(CODES)
    times = BLOCK // 128
    code, event, end = labs[0], labs[1], labs[2]
    own_code = jnp.where(event >= 0, code, -1.0)

    def widen(tile):
        return jnp.concatenate([tile] * times, 1)

    def block_ids(b):
        return (b * BLOCK + lax.broadcasted_iota(jnp.int32, (1, BLOCK), 1)).astype(F32)

    def block_at(b):
        return pl.ds(pl.multiple_of(b * BLOCK, BLOCK), BLOCK)

    own_row[...] = jnp.zeros_like(own_row)

    @pl.loop(0, CODES // BLOCK)
    def _(b):
        hot = jnp.where(widen(own_code) == block_ids(b), 1.0, 0.0).astype(BF16)
        own_row[...] += mm(hot, table_ref[block_at(b), :])

    for p in range(PIECES):
        at_code = jnp.sum(reps[p].astype(F32) * own_row[...], -1, keepdims=True)
        value = jnp.exp2(at_code * LOG2E - log_codes) - 1.0
        fix[p] = jnp.where(event == p, value, 0.0)

    greps[...] = jnp.zeros_like(greps)

    @pl.loop(0, CODES // BLOCK)
    def _(b):
        tab = table_ref[block_at(b), :]
        ids = block_ids(b)

        def weights(p, logits):
            live = widen(jnp.where(end >= p, -log_codes, -1e30))
            e = jnp.exp2(logits * LOG2E + live)
            act = widen(jnp.where(event <= p, own_code, -1.0))
            return jnp.where(act == ids, widen(fix[p]), e).astype(BF16)

        logits = mm_nt(reps[0], tab)
        total = jnp.zeros((R, BLOCK), F32)
        for p in range(PIECES):
            after = mm_nt(reps[p + 1], tab) if p + 1 < PIECES else None
            g = weights(p, logits)
            greps[p] += mm(g, tab)
            total = total + mm(reps_t[p], g)
            logits = after
        turned = total.T.astype(BF16).reshape(BLOCK // 128, 128, 128)
        src_t[pl.ds(b * (BLOCK // 128), BLOCK // 128)] = turned
        table_core(b).start()

        @pl.when(b > 0)
        def _():
            table_to_ring(b - 1)

    table_to_ring(3)

    for p in range(PIECES):
        glow[:, p * 128 : p * 128 + 128] = greps[p].astype(BF16)

    turned_p[...] = mm_nt(perm[...], hidden[...]).astype(BF16)
    for j in range(4):
        cols = slice(j * 256, j * 256 + 256)
        src_p[:, :, j * 128 : j * 128 + 128] = stack_halves(mm(turned_p[...], glow[:, cols]))
    begin("p")

    for j in range(3):
        cols = slice(j * 256, j * 256 + 256)
        ghid[:, cols] = mm_nt(glow[...], wpiece[cols, :]).astype(BF16)

    ctx_t = ctx[...].T
    for j in range(3):
        cols = slice(j * 256, j * 256 + 256)
        src_o[:, :, j * 128 : j * 128 + 128] = stack_halves(mm(ctx_t, ghid[:, cols]))
    begin("o")
    to_first_ring("p")

    for j in range(3):
        cols = slice(j * 256, j * 256 + 256)
        gctx[:, cols] = mm_nt(ghid[...], wout[cols, :]).astype(BF16)
    to_first_ring("o")
    normed_t[...] = normed[...].T
    turned_p[...] = mm_nt(perm[...], normed[...]).astype(BF16)
    to_second_ring("t")

    def backward_pair(p):
        q = qkv[p]
        k = qkv[PAIRS + p]
        v = qkv[2 * PAIRS + p]
        g = gctx[:, lanes(p)]
        gh = [head_part(g[span(rb)], head) for rb, head in TODO]
        low = [prob[p, head, span(rb), : far(rb)] for rb, head in TODO]
        dp = [mm_nt(a, v[: far(rb)]) for (rb, head), a in zip(TODO, gh)]
        inner = [jnp.sum(a * b.astype(F32), -1, keepdims=True) for a, b in zip(dp, low)]
        ds = [(b.astype(F32) * (a - i)).astype(BF16) for a, b, i in zip(dp, low, inner)]
        cat = lambda a, i: jnp.concatenate([a[i], a[i + 1]], 0)
        dv = [mm_tn(cat(low, i), cat(gh, i)) for i in (0, 2)]
        dq = [mm(a, k[: far(rb)]) for (rb, head), a in zip(TODO, ds)]
        qh = [head_part(q[span(rb)], head) for rb, head in TODO]
        dk = [mm_tn(cat(ds, i), cat(qh, i)) for i in (0, 2)]
        for rb in range(2):
            both = jnp.where(low_lanes, dq[2 * rb], dq[2 * rb + 1]) * 0.125
            dqkv[span(rb), lanes(p)] = both.astype(BF16)
        for at, parts in ((PAIRS, dk), (2 * PAIRS, dv)):
            wide = parts[1]
            dqkv[:256, lanes(at + p)] = (wide[:256] + parts[0]).astype(BF16)
            dqkv[256:, lanes(at + p)] = wide[256:].astype(BF16)

    def backward_step(s):
        pl.loop(2 * s, 2 * s + 2, unroll=2)(backward_pair)

    def qkv_step(s):
        for part in (2, 0, 1):
            cols = slice(part * D + s * 256, part * D + s * 256 + 256)
            left = turned_p if part == 2 else normed_t
            res = stack_halves(mm(left[...], dqkv[:, cols]))
            if part == 2:
                src_v[s] = res
                begin("v%d" % s)
            else:
                src_a[s, :, :, part * 128 : part * 128 + 128] = res
        begin("a%d" % s)

    def each(stage, s):
        for part in "va":
            stage(part + str(s))

    backward_step(0)
    qkv_step(0)
    to_last("t")
    backward_step(1)
    each(to_first_ring, 0)
    qkv_step(1)
    backward_step(2)
    each(to_first_ring, 1)
    qkv_step(2)
    to_second_ring("p")
    to_second_ring("o")

    for j in range(3):
        cols = slice(j * 256, j * 256 + 256)
        gnorm[:, cols] = mm_nt(dqkv[...], wqkv[cols, :])

    x = landed[:, :, :D].reshape(ROWS, D).astype(F32)
    inv_rms = lax.rsqrt(jnp.mean(x * x, -1, keepdims=True) + EPSILON)
    x_hat = x * inv_rms
    gn = gnorm[...]
    ggain = jnp.sum(gn * x_hat, 0, keepdims=True)
    feature = lax.broadcasted_iota(jnp.int32, (ROWS, D), 1)
    block = lax.broadcasted_iota(jnp.int32, (ROWS, D), 0) // SLOT
    spread = jnp.where(feature // 24 == block, ggain, 0.0).astype(BF16)
    pick = lax.broadcasted_iota(jnp.int32, (D, 128), 0) % 24
    pick = jnp.where(pick == lax.broadcasted_iota(jnp.int32, (D, 128), 1), 1.0, 0.0).astype(BF16)
    src_g[...] = mm(spread, pick).astype(BF16).reshape(WIN, SLOT, 128)
    begin("g")
    each(to_first_ring, 2)

    gh = gn * gain
    gx = inv_rms * (gh - x_hat * jnp.mean(gh * x_hat, -1, keepdims=True))
    gb = (gx + ghid[...].astype(F32)).astype(BF16)
    rows_out[...] = gb.reshape(WIN, SLOT, D)
    to_first_ring("g")
    exchange_rows(rows_out, returned, back_send, back_recv, me, 1, 12)
    each(to_second_ring, 0)
    exchange_rows(rows_out, returned, back_send, back_recv, me, 12, 22)
    to_last("p")
    to_last("o")
    each(to_second_ring, 1)
    exchange_rows(rows_out, returned, back_send, back_recv, me, 22, WIN)
    returned[me] = rows_out[me]
    to_second_ring("g")
    each(to_last, 0)
    each(to_second_ring, 2)
    each(to_last, 1)
    to_last("g")
    for name in ("t", "p", "o"):
        finish(name)
    each(finish, 0)
    each(to_last, 2)
    each(finish, 1)
    wait_rows(rows_out, returned, back_send, back_recv, me)
    rows_ref[...] = mm_tn(hot_ref[...], returned[...].reshape(ROWS, D)).astype(BF16)
    finish("g")
    each(finish, 2)


def step(events, labels, counts, gain, w_qkv, w_out, w_piece, table):
    vmem = pl.BlockSpec(memory_space=pltpu.VMEM)
    scratch = [
        pltpu.VMEM((D, 3 * D), BF16),
        pltpu.VMEM((D, D), BF16),
        pltpu.VMEM((D, PIECES * R), BF16),
        pltpu.VMEM((CODES, R), BF16),
        pltpu.SemaphoreType.DMA((4,)),
        pltpu.VMEM((ROWS, EVENTS), BF16),
        pltpu.VMEM((WIN, SLOT, WIDE), BF16),
        pltpu.VMEM((WIN, SLOT, WIDE), BF16),
        pltpu.VMEM((WIN, SLOT, D), BF16),
        pltpu.VMEM((WIN, SLOT, D), BF16),
        pltpu.SemaphoreType.DMA((WIN,)),
        pltpu.SemaphoreType.DMA((WIN,)),
        pltpu.SemaphoreType.DMA((WIN,)),
        pltpu.SemaphoreType.DMA((WIN,)),
        pltpu.SemaphoreType.DMA((N_ITEMS, 10)),
        pltpu.SemaphoreType.DMA((N_ITEMS, 10)),
        pltpu.SemaphoreType.DMA((4, 4)),
        pltpu.SemaphoreType.DMA((4, 4)),
        pltpu.VMEM((WIN, 128, 128), BF16),
        pltpu.VMEM((WIN, 48, 512), BF16),
        pltpu.VMEM((WIN, 48, 384), BF16),
        pltpu.VMEM((3, WIN, 48, 256), BF16),
        pltpu.VMEM((3, WIN, 48, 128), BF16),
        pltpu.VMEM((WIN, SLOT, 128), BF16),
        pltpu.VMEM((D, D), BF16),
        pltpu.VMEM((D, ROWS), BF16),
        pltpu.VMEM((2, 32, 512), F32),
        pltpu.VMEM((ROWS, D), BF16),
        pltpu.VMEM((D, ROWS), BF16),
        pltpu.VMEM((18, ROWS, 128), BF16),
        pltpu.VMEM((PAIRS, 2, ROWS, ROWS), BF16),
        pltpu.VMEM((ROWS, D), BF16),
        pltpu.VMEM((ROWS, D), BF16),
        pltpu.VMEM((PIECES, ROWS, R), BF16),
        pltpu.VMEM((PIECES, R, ROWS), BF16),
        pltpu.VMEM((PIECES, ROWS, R), F32),
        pltpu.VMEM((ROWS, R), F32),
        pltpu.VMEM((PIECES, ROWS, 128), F32),
        pltpu.VMEM((ROWS, PIECES * R), BF16),
        pltpu.VMEM((ROWS, D), BF16),
        pltpu.VMEM((ROWS, D), BF16),
        pltpu.VMEM((ROWS, 3 * D), BF16),
        pltpu.VMEM((ROWS, ROWS), F32),
        pltpu.VMEM((3, ROWS, 128), F32),
        pltpu.VMEM((ROWS, D), F32),
    ]
    for name, rows, width, order in ITEMS:
        last = 32 if name == "t" else 16
        scratch += [
            pltpu.VMEM((4, 4, rows, width), BF16),
            pltpu.VMEM((3, 4, rows, width), BF16),
            pltpu.VMEM((4, rows, width), BF16),
            pltpu.VMEM((3, rows, width), BF16),
            pltpu.VMEM((4, last, width), BF16),
            pltpu.VMEM((3, last, width), BF16),
        ]
    return pl.pallas_call(
        step_kernel,
        out_shape=(
            jax.ShapeDtypeStruct((EVENTS, D), BF16),
            jax.ShapeDtypeStruct((8, 128), F32),
            jax.ShapeDtypeStruct((6, 3 * D), F32),
            jax.ShapeDtypeStruct((6, D), F32),
            jax.ShapeDtypeStruct((6, PIECES * R), F32),
            jax.ShapeDtypeStruct((32, R), F32),
        ),
        in_specs=[vmem] * 4 + [pl.BlockSpec(memory_space=pl.ANY)] * 4,
        out_specs=(vmem,) * 6,
        scratch_shapes=scratch,
        compiler_params=pltpu.CompilerParams(
            collective_id=1, has_side_effects=True, vmem_limit_bytes=63 * 1024 * 1024
        ),
        name="step",
    )(events, labels, counts, gain, w_qkv, w_out, w_piece, table)


def result_kernel(*refs):
    for src, dst in zip(refs[:5], refs[6:11]):
        dst[...] = src[...]
    refs[11][...] = refs[5][0, :6]


def results(rows, g_qkv, g_out, g_piece, g_table, gain):
    vmem = pl.BlockSpec(memory_space=pltpu.VMEM)
    like = [jax.ShapeDtypeStruct(a.shape, a.dtype) for a in (rows, g_qkv, g_out, g_piece, g_table)]
    return pl.pallas_call(
        result_kernel,
        out_shape=(*like, jax.ShapeDtypeStruct((6,), F32)),
        in_specs=[vmem] * 6,
        out_specs=(vmem,) * 6,
        name="results",
    )(rows, g_qkv, g_out, g_piece, g_table, gain)


def body(
    events,
    send_counts,
    patient_ids,
    codes,
    event_piece,
    censor_piece,
    norm_gain,
    w_qkv,
    w_out,
    w_piece,
    code_table,
):
    labels = jnp.concatenate([patient_ids[0], codes[0], event_piece[0], censor_piece[0]], 0)
    rows, gain, g_qkv, g_out, g_piece, g_table = step(
        events[0, 0], labels, send_counts[0], norm_gain[None], w_qkv, w_out, w_piece, code_table
    )
    rows, g_qkv, g_out, g_piece, g_table, g_gain = results(rows, g_qkv, g_out, g_piece, g_table, gain)
    return (rows[None, None], g_gain, g_qkv, g_out, g_piece, g_table)


def solution(mesh):
    split = P("win", "rep")
    return jax.shard_map(
        body,
        mesh=mesh,
        in_specs=(split,) * 6 + (P(),) * 5,
        out_specs=(split,) + (P(("win", "rep")),) * 5,
        check_vma=False,
    )
```

```python
import functools
import math

import jax
import jax.numpy as jnp
from jax import lax
from jax.experimental import pallas as pl
from jax.experimental.pallas import tpu as pltpu
from jax.sharding import PartitionSpec as P

HEADS = 12
EPSILON = 1e-05
MESH = pl.DeviceIdType.MESH

D = 768
PAIRS = 6
PIECES = 8
CODES = 4096
R = 128
ROWS = 512
EVENTS = 256
WIN = 32
SLOT = 16
LAB = 128
WIDE = D + LAB
BLOCK = 1024
LOG2E = math.log2(math.e)

F32 = jnp.float32
BF16 = jnp.bfloat16

NT = (((1,), (1,)), ((), ()))
TN = (((0,), (0,)), ((), ()))


def mm(a, b):
    return jnp.dot(a, b, preferred_element_type=F32)


def mm_nt(a, b):
    return lax.dot_general(a, b, NT, preferred_element_type=F32)


def mm_tn(a, b):
    return lax.dot_general(a, b, TN, preferred_element_type=F32)


def exchange_rows(src_ref, dst_ref, send_sem, recv_sem, me, low=1, high=WIN):
    @pl.loop(low, high)
    def _(k):
        peer = lax.rem(me + k, WIN)
        pltpu.make_async_remote_copy(
            src_ref=src_ref.at[peer],
            dst_ref=dst_ref.at[me],
            send_sem=send_sem.at[k],
            recv_sem=recv_sem.at[k],
            device_id={"win": peer},
            device_id_type=MESH,
        ).start()


def wait_rows(src_ref, dst_ref, send_sem, recv_sem, me):
    @pl.loop(1, WIN)
    def _(k):
        sender = lax.rem(me + WIN - k, WIN)
        pltpu.make_async_remote_copy(
            src_ref=src_ref.at[me],
            dst_ref=dst_ref.at[sender],
            send_sem=send_sem.at[k],
            recv_sem=recv_sem.at[k],
            device_id={"win": sender},
            device_id_type=MESH,
        ).wait()


def stack_halves(res):
    tiles = res.reshape(WIN, 3, 8, 256)
    both = jnp.concatenate([tiles[..., :128], tiles[..., 128:]], 2)
    return both.reshape(WIN, 48, 128).astype(BF16)


TODO = [(rb, head) for rb in range(2) for head in range(2)]


def span(rb):
    return slice(rb * 256, rb * 256 + 256)


def far(rb):
    return rb * 256 + 256


def lanes(index):
    return pl.ds(pl.multiple_of(index * 128, 128), 128)


ITEMS = (
    ("t", 128, 128, "zxy"),
    ("p", 48, 512, "yxz"),
    ("o", 48, 384, "zxy"),
    ("a0", 48, 256, "xzy"),
    ("v0", 48, 128, "yxz"),
    ("a1", 48, 256, "zxy"),
    ("v1", 48, 128, "yxz"),
    ("a2", 48, 256, "xzy"),
    ("v2", 48, 128, "yxz"),
    ("g", 16, 128, "zxy"),
)
N_ITEMS = len(ITEMS)
INDEX = {item[0]: i for i, item in enumerate(ITEMS)}


def remote(src, dst, sems, index, where):
    return pltpu.make_async_remote_copy(
        src_ref=src,
        dst_ref=dst,
        send_sem=sems[0].at[index],
        recv_sem=sems[1].at[index],
        device_id=where,
        device_id_type=MESH,
    )


def step_kernel(
    ev_ref,
    lab_ref,
    cnt_ref,
    gain_ref,
    wqkv_any,
    wout_any,
    wpiece_any,
    table_any,
    rows_ref,
    gain_out,
    qkv_ref,
    out_ref,
    piece_ref,
    tab_ref,
    wqkv,
    wout,
    wpiece,
    table_ref,
    load_sem,
    hot_ref,
    packed,
    landed,
    rows_out,
    returned,
    there_send,
    there_recv,
    back_send,
    back_recv,
    sum_send,
    sum_recv,
    tab_send,
    tab_recv,
    src_t,
    src_p,
    src_o,
    src_a,
    src_v,
    src_g,
    perm,
    turned_p,
    tiles,
    normed,
    normed_t,
    qkv,
    prob,
    ctx,
    hidden,
    reps,
    reps_t,
    greps,
    own_row,
    fix,
    glow,
    ghid,
    gctx,
    dqkv,
    bias,
    labs,
    gnorm,
    *spare,
):
    bufs = [spare[6 * i : 6 * i + 6] for i in range(N_ITEMS)]
    sems = (sum_send, sum_recv)
    me = lax.axis_index("win")
    y = lax.axis_index("rep")
    core = lax.rem(me, 2)
    z_at = lax.rem(me // 2, 4)
    x_at = me // 8

    barrier = pltpu.get_barrier_semaphore()

    @pl.loop(1, WIN)
    def _(k):
        pl.semaphore_signal(
            barrier, inc=1, device_id={"win": lax.rem(me + k, WIN)}, device_id_type=MESH
        )

    @pl.loop(1, 4)
    def _(k):
        pl.semaphore_signal(
            barrier, inc=1, device_id={"rep": lax.rem(y + k, 4)}, device_id_type=MESH
        )

    loads = [
        pltpu.make_async_copy(src, dst, load_sem.at[i])
        for i, (src, dst) in enumerate(
            ((wqkv_any, wqkv), (wout_any, wout), (wpiece_any, wpiece), (table_any, table_ref))
        )
    ]
    for load in loads:
        load.start()

    counts = cnt_ref[...].astype(F32)
    row = lax.broadcasted_iota(jnp.int32, (ROWS, WIN), 0)
    owner = lax.broadcasted_iota(jnp.int32, (ROWS, WIN), 1)
    row_owner = row // SLOT
    mine = jnp.sum(jnp.where(owner == row_owner, counts, 0.0), 1, keepdims=True)
    start = jnp.sum(jnp.where(owner < row_owner, counts, 0.0), 1, keepdims=True)
    offset = (lax.broadcasted_iota(jnp.int32, (ROWS, 1), 0) % SLOT).astype(F32)
    place = lax.broadcasted_iota(jnp.int32, (ROWS, EVENTS), 1).astype(F32)
    wanted = jnp.where(offset < mine, start + offset, -1.0)
    hot = jnp.where(place == wanted, 1.0, 0.0).astype(BF16)
    hot_ref[...] = hot
    packed[:, :, :D] = mm(hot, ev_ref[...]).astype(BF16).reshape(WIN, SLOT, D)

    lab = lab_ref[...]
    high = lab[1:2] // 64
    rows = [lab[0:1], high, lab[1:2] - high * 64, lab[2:3], jnp.maximum(lab[2:3], lab[3:4])]
    rows.append(jnp.ones((1, EVENTS), jnp.int32))
    rows.append(jnp.zeros((2, EVENTS), jnp.int32))
    table = jnp.concatenate(rows, 0).astype(F32)
    table = jnp.concatenate([table, jnp.zeros((LAB - 8, EVENTS), F32)], 0).astype(BF16)
    packed[:, :, D:] = mm_nt(hot, table).astype(BF16).reshape(WIN, SLOT, LAB)

    pl.semaphore_wait(barrier, WIN - 1 + 3)
    exchange_rows(packed, landed, there_send, there_recv, me)
    landed[me] = packed[me]

    at = lax.broadcasted_iota(jnp.int32, (D, 1), 0)
    group, inner = at // 24, at % 24
    z_of, r_of = inner // 6, inner % 6
    y_of, x_of, core_of = group // 8, (group // 2) % 4, group % 2
    feature = ((x_of * 4 + z_of) * 2 + core_of) * 24 + y_of * 6 + r_of
    chosen = lax.broadcasted_iota(jnp.int32, (D, D), 1) == feature
    perm[...] = jnp.where(chosen, 1.0, 0.0).astype(BF16)

    wait_rows(packed, landed, there_send, there_recv, me)

    sources = {"t": src_t, "p": src_p, "o": src_o, "g": src_g}
    for s in range(3):
        sources["a%d" % s] = src_a.at[s]
        sources["v%d" % s] = src_v.at[s]
    mine_at = {"x": x_at, "y": y, "z": z_at}

    def place_of(axis, k):
        return lax.rem(mine_at[axis] + k, 4)

    def device_of(axis, k):
        if axis == "x":
            return {"win": place_of("x", k) * 8 + z_at * 2 + core}
        if axis == "z":
            return {"win": x_at * 8 + place_of("z", k) * 2 + core}
        return {"rep": place_of("y", k)}

    def blocked(name):
        _, rows, width, _ = ITEMS[INDEX[name]]
        return sources[name].reshape(4, 4, 2, rows, width)

    def buf(name):
        return bufs[INDEX[name]]

    def core_copy(name):
        i = INDEX[name]
        return remote(
            blocked(name).at[:, :, 1 - core], buf(name)[0], sems, (i, 0), {"win": me + 1 - 2 * core}
        )

    def block_of(ref, order, first, second=None):
        if order in ("xzy", "yxz"):
            return ref.at[first] if second is None else ref.at[first, second]
        return ref.at[:, first] if second is None else ref.at[second, first]

    def ring_copy(name, step, k):
        i = INDEX[name]
        order = ITEMS[i][3]
        if step == 0:
            src = block_of(buf(name)[0], order, place_of(order[0], k))
        else:
            src = buf(name)[2].at[place_of(order[1], k)]
        return remote(
            src,
            buf(name)[1 + 2 * step].at[k - 1],
            sems,
            (i, 1 + 3 * step + k - 1),
            device_of(order[step], k),
        )

    def last_copy(name, k):
        axis = ITEMS[INDEX[name]][3][2]
        return remote(
            buf(name)[4].at[place_of(axis, k)],
            buf(name)[5].at[k - 1],
            sems,
            (INDEX[name], 7 + k - 1),
            device_of(axis, k),
        )

    def table_core(b):
        return remote(
            blocked("t").at[b, :, 1 - core],
            buf("t")[0].at[b],
            (tab_send, tab_recv),
            (b, 0),
            {"win": me + 1 - 2 * core},
        )

    def table_ring(b, k):
        return remote(
            buf("t")[0].at[b, place_of("z", k)],
            buf("t")[1].at[k - 1, b],
            (tab_send, tab_recv),
            (b, k),
            device_of("z", k),
        )

    def table_to_ring(b):
        table_core(b).wait()
        src, got = blocked("t"), buf("t")[0]
        for c in range(4):
            got[b, c] = (src[b, c, core].astype(F32) + got[b, c].astype(F32)).astype(BF16)
        for k in (2, 1, 3):
            table_ring(b, k).start()

    def begin(name):
        core_copy(name).start()

    def to_first_ring(name):
        core_copy(name).wait()
        src, got = blocked(name), buf(name)[0]
        for a in range(4):

            @pl.loop(0, 4)
            def _(b):
                got[a, b] = (src[a, b, core].astype(F32) + got[a, b].astype(F32)).astype(BF16)

        for k in (2, 1, 3):
            ring_copy(name, 0, k).start()

    def to_second_ring(name):
        order = ITEMS[INDEX[name]][3]
        if name == "t":

            @pl.loop(0, 4)
            def _(b):
                for k in (2, 1, 3):
                    table_ring(b, k).wait()
        else:
            for k in (2, 1, 3):
                ring_copy(name, 0, k).wait()
        mine, got, acc = buf(name)[0], buf(name)[1], buf(name)[2]

        @pl.loop(0, 4)
        def _(b):
            total = block_of(mine, order, place_of(order[0], 0), b)[...].astype(F32)
            for k in range(3):
                total += got[k, b].astype(F32)
            acc[b] = total.astype(BF16)

        for k in (2, 1, 3):
            ring_copy(name, 1, k).start()

    def to_last(name):
        _, rows, width, order = ITEMS[INDEX[name]]
        for k in (2, 1, 3):
            ring_copy(name, 1, k).wait()
        got = buf(name)[3]
        total = buf(name)[2][place_of(order[1], 0)].astype(F32)
        for k in range(3):
            total += got[k].astype(F32)
        low = buf(name)[4]
        if name == "t":
            low[...] = total.astype(BF16).reshape(4, 32, 128)
        elif name == "g":
            for yy in range(4):
                low[yy] = (pltpu.roll(total, 128 - 6 * yy, 1) if yy else total).astype(BF16)
        else:
            for half in range(2):
                for t in range(3):
                    at = t * 16 + half * 8
                    tiles[half, t * 8 : t * 8 + 8, :width] = total[at : at + 8]
            for yy in range(4):
                both = jnp.concatenate(
                    [tiles[0, 6 * yy : 6 * yy + 8, :width], tiles[1, 6 * yy : 6 * yy + 8, :width]], 0
                )
                low[yy] = both.astype(BF16)
        for k in (2, 1, 3):
            last_copy(name, k).start()

    def finish(name):
        _, rows, width, order = ITEMS[INDEX[name]]
        for k in (2, 1, 3):
            last_copy(name, k).wait()
        got = buf(name)[5]
        total = buf(name)[4][place_of(order[2], 0)].astype(F32)
        for k in range(3):
            total += got[k].astype(F32)
        total = total * (1.0 / math.sqrt(EVENTS * WIN * 4))
        if name == "t":
            tab_ref[...] = total
        elif name == "g":
            gain_out[...] = total[:8]
        else:
            for u in range(width // 128):
                if name == "p":
                    dst, at = piece_ref, u * 256
                elif name == "o":
                    dst, at = out_ref, u * 256
                else:
                    part = u if name[0] == "a" else 2
                    dst, at = qkv_ref, part * D + int(name[1]) * 256
                us = slice(u * 128, u * 128 + 128)
                dst[:, at : at + 128] = total[:6, us]
                dst[:, at + 128 : at + 256] = total[8:14, us]

    gain = gain_ref[...]
    lab = landed[:, :, D:].reshape(ROWS, LAB).astype(F32)
    valid = lab[:, 5:6] > 0.5
    patient = jnp.where(valid, lab[:, 0:1], -1.0)
    labs[0] = jnp.broadcast_to(lab[:, 1:2] * 64.0 + lab[:, 2:3], (ROWS, 128))
    labs[1] = jnp.broadcast_to(jnp.where(valid, lab[:, 3:4], -1.0), (ROWS, 128))
    labs[2] = jnp.broadcast_to(jnp.where(valid, lab[:, 4:5], -1.0), (ROWS, 128))

    lab_t = lab.T
    patient_row = jnp.where(lab_t[5:6] > 0.5, lab_t[0:1], -1.0)
    row = lax.broadcasted_iota(jnp.int32, (ROWS, ROWS), 0)
    col = lax.broadcasted_iota(jnp.int32, (ROWS, ROWS), 1)
    allowed = ((patient == patient_row) & (col <= row)) | (col == row)
    bias[...] = jnp.where(allowed, 0.0, -1e30)

    x = landed[:, :, :D].reshape(ROWS, D).astype(F32)
    inv_rms = lax.rsqrt(jnp.mean(x * x, -1, keepdims=True) + EPSILON)
    normed[...] = (x * inv_rms * gain).astype(BF16)

    loads[0].wait()

    @pl.loop(0, 9)
    def _(j):
        cols = pl.ds(pl.multiple_of(j * 256, 256), 256)
        res = mm(normed[...], wqkv[:, cols])
        scale = jnp.where(j < 3, 0.125, 1.0)
        res = (res * scale).astype(BF16)
        qkv[2 * j] = res[:, :128]
        qkv[2 * j + 1] = res[:, 128:]

    low_lanes = lax.broadcasted_iota(jnp.int32, (1, 128), 1) < 64

    def head_part(value, head):
        zero = jnp.zeros((), value.dtype)
        return jnp.where(low_lanes, value, zero) if head == 0 else jnp.where(low_lanes, zero, value)

    @pl.loop(0, PAIRS, unroll=2)
    def _(p):
        q = qkv[p]
        k = qkv[PAIRS + p]
        v = qkv[2 * PAIRS + p]
        s = [mm_nt(head_part(q[span(rb)], head), k[: far(rb)]) + bias[span(rb), : far(rb)] for rb, head in TODO]
        top = [jnp.max(a, -1, keepdims=True) for a in s]
        w = [jnp.exp(a - m) for a, m in zip(s, top)]
        inv = [1.0 / jnp.sum(a, -1, keepdims=True) for a in w]
        pr = [(a * i).astype(BF16) for a, i in zip(w, inv)]
        for (rb, head), a in zip(TODO, pr):
            prob[p, head, span(rb), : far(rb)] = a
        got = [mm(a, v[: far(rb)]) for (rb, head), a in zip(TODO, pr)]
        for rb in range(2):
            ctx[span(rb), lanes(p)] = jnp.where(low_lanes, got[2 * rb], got[2 * rb + 1]).astype(BF16)

    loads[1].wait()

    @pl.loop(0, 3)
    def _(j):
        cols = pl.ds(pl.multiple_of(j * 256, 256), 256)
        res = mm(ctx[...], wout[:, cols])
        hidden[:, cols] = (landed[:, :, cols].reshape(ROWS, 256).astype(F32) + res).astype(BF16)

    loads[2].wait()

    @pl.loop(0, 4)
    def _(j):
        cols = pl.ds(pl.multiple_of(j * 256, 256), 256)
        res = mm(hidden[...], wpiece[:, cols])
        for i in range(2):
            part = res[:, i * 128 : i * 128 + 128]
            reps[2 * j + i] = part.astype(BF16)
            reps_t[2 * j + i] = part.T.astype(BF16)

    loads[3].wait()

    log_codes = math.log2(CODES)
    times = BLOCK // 128
    code, event, end = labs[0], labs[1], labs[2]
    own_code = jnp.where(event >= 0, code, -1.0)

    def widen(tile):
        return jnp.concatenate([tile] * times, 1)

    def block_ids(b):
        return (b * BLOCK + lax.broadcasted_iota(jnp.int32, (1, BLOCK), 1)).astype(F32)

    def block_at(b):
        return pl.ds(pl.multiple_of(b * BLOCK, BLOCK), BLOCK)

    own_row[...] = jnp.zeros_like(own_row)

    @pl.loop(0, CODES // BLOCK)
    def _(b):
        hot = jnp.where(widen(own_code) == block_ids(b), 1.0, 0.0).astype(BF16)
        own_row[...] += mm(hot, table_ref[block_at(b), :])

    for p in range(PIECES):
        at_code = jnp.sum(reps[p].astype(F32) * own_row[...], -1, keepdims=True)
        value = jnp.exp2(at_code * LOG2E - log_codes) - 1.0
        fix[p] = jnp.where(event == p, value, 0.0)

    greps[...] = jnp.zeros_like(greps)

    @pl.loop(0, CODES // BLOCK)
    def _(b):
        tab = table_ref[block_at(b), :]
        ids = block_ids(b)

        def weights(p, logits):
            live = widen(jnp.where(end >= p, -log_codes, -1e30))
            e = jnp.exp2(logits * LOG2E + live)
            act = widen(jnp.where(event <= p, own_code, -1.0))
            return jnp.where(act == ids, widen(fix[p]), e).astype(BF16)

        logits = mm_nt(reps[0], tab)
        total = jnp.zeros((R, BLOCK), F32)
        for p in range(PIECES):
            after = mm_nt(reps[p + 1], tab) if p + 1 < PIECES else None
            g = weights(p, logits)
            greps[p] += mm(g, tab)
            total = total + mm(reps_t[p], g)
            logits = after
        turned = total.T.astype(BF16).reshape(BLOCK // 128, 128, 128)
        src_t[pl.ds(b * (BLOCK // 128), BLOCK // 128)] = turned
        table_core(b).start()

        @pl.when(b > 0)
        def _():
            table_to_ring(b - 1)

    table_to_ring(3)

    for p in range(PIECES):
        glow[:, p * 128 : p * 128 + 128] = greps[p].astype(BF16)

    turned_p[...] = mm_nt(perm[...], hidden[...]).astype(BF16)
    for j in range(4):
        cols = slice(j * 256, j * 256 + 256)
        src_p[:, :, j * 128 : j * 128 + 128] = stack_halves(mm(turned_p[...], glow[:, cols]))
    begin("p")

    for j in range(3):
        cols = slice(j * 256, j * 256 + 256)
        ghid[:, cols] = mm_nt(glow[...], wpiece[cols, :]).astype(BF16)

    ctx_t = ctx[...].T
    for j in range(3):
        cols = slice(j * 256, j * 256 + 256)
        src_o[:, :, j * 128 : j * 128 + 128] = stack_halves(mm(ctx_t, ghid[:, cols]))
    begin("o")
    to_first_ring("p")

    for j in range(3):
        cols = slice(j * 256, j * 256 + 256)
        gctx[:, cols] = mm_nt(ghid[...], wout[cols, :]).astype(BF16)
    to_first_ring("o")
    normed_t[...] = normed[...].T
    turned_p[...] = mm_nt(perm[...], normed[...]).astype(BF16)
    to_second_ring("t")

    def backward_pair(p):
        q = qkv[p]
        k = qkv[PAIRS + p]
        v = qkv[2 * PAIRS + p]
        g = gctx[:, lanes(p)]
        gh = [head_part(g[span(rb)], head) for rb, head in TODO]
        low = [prob[p, head, span(rb), : far(rb)] for rb, head in TODO]
        dp = [mm_nt(a, v[: far(rb)]) for (rb, head), a in zip(TODO, gh)]
        inner = [jnp.sum(a * b.astype(F32), -1, keepdims=True) for a, b in zip(dp, low)]
        ds = [(b.astype(F32) * (a - i)).astype(BF16) for a, b, i in zip(dp, low, inner)]
        cat = lambda a, i: jnp.concatenate([a[i], a[i + 1]], 0)
        dv = [mm_tn(cat(low, i), cat(gh, i)) for i in (0, 2)]
        dq = [mm(a, k[: far(rb)]) for (rb, head), a in zip(TODO, ds)]
        qh = [head_part(q[span(rb)], head) for rb, head in TODO]
        dk = [mm_tn(cat(ds, i), cat(qh, i)) for i in (0, 2)]
        for rb in range(2):
            both = jnp.where(low_lanes, dq[2 * rb], dq[2 * rb + 1]) * 0.125
            dqkv[span(rb), lanes(p)] = both.astype(BF16)
        for at, parts in ((PAIRS, dk), (2 * PAIRS, dv)):
            wide = parts[1]
            dqkv[:256, lanes(at + p)] = (wide[:256] + parts[0]).astype(BF16)
            dqkv[256:, lanes(at + p)] = wide[256:].astype(BF16)

    def backward_step(s):
        pl.loop(2 * s, 2 * s + 2, unroll=2)(backward_pair)

    def qkv_step(s):
        for part in (2, 0, 1):
            cols = slice(part * D + s * 256, part * D + s * 256 + 256)
            left = turned_p if part == 2 else normed_t
            res = stack_halves(mm(left[...], dqkv[:, cols]))
            if part == 2:
                src_v[s] = res
                begin("v%d" % s)
            else:
                src_a[s, :, :, part * 128 : part * 128 + 128] = res
        begin("a%d" % s)

    def each(stage, s):
        for part in "va":
            stage(part + str(s))

    backward_step(0)
    qkv_step(0)
    to_last("t")
    backward_step(1)
    each(to_first_ring, 0)
    qkv_step(1)
    backward_step(2)
    each(to_first_ring, 1)
    qkv_step(2)
    to_second_ring("p")
    to_second_ring("o")

    for j in range(3):
        cols = slice(j * 256, j * 256 + 256)
        gnorm[:, cols] = mm_nt(dqkv[...], wqkv[cols, :])

    x = landed[:, :, :D].reshape(ROWS, D).astype(F32)
    inv_rms = lax.rsqrt(jnp.mean(x * x, -1, keepdims=True) + EPSILON)
    x_hat = x * inv_rms
    gn = gnorm[...]
    ggain = jnp.sum(gn * x_hat, 0, keepdims=True)
    feature = lax.broadcasted_iota(jnp.int32, (ROWS, D), 1)
    block = lax.broadcasted_iota(jnp.int32, (ROWS, D), 0) // SLOT
    spread = jnp.where(feature // 24 == block, ggain, 0.0).astype(BF16)
    pick = lax.broadcasted_iota(jnp.int32, (D, 128), 0) % 24
    pick = jnp.where(pick == lax.broadcasted_iota(jnp.int32, (D, 128), 1), 1.0, 0.0).astype(BF16)
    src_g[...] = mm(spread, pick).astype(BF16).reshape(WIN, SLOT, 128)
    begin("g")
    each(to_first_ring, 2)
    each(to_second_ring, 0)

    gh = gn * gain
    gx = inv_rms * (gh - x_hat * jnp.mean(gh * x_hat, -1, keepdims=True))
    gb = (gx + ghid[...].astype(F32)).astype(BF16)
    rows_out[...] = gb.reshape(WIN, SLOT, D)
    to_last("p")
    to_last("o")
    to_first_ring("g")
    exchange_rows(rows_out, returned, back_send, back_recv, me, 1, 16)
    each(to_second_ring, 1)
    exchange_rows(rows_out, returned, back_send, back_recv, me, 16, WIN)
    returned[me] = rows_out[me]
    to_second_ring("g")
    each(to_last, 0)
    each(to_second_ring, 2)
    each(to_last, 1)
    to_last("g")
    for name in ("t", "p", "o"):
        finish(name)
    each(finish, 0)
    each(to_last, 2)
    each(finish, 1)
    wait_rows(rows_out, returned, back_send, back_recv, me)
    rows_ref[...] = mm_tn(hot_ref[...], returned[...].reshape(ROWS, D)).astype(BF16)
    finish("g")
    each(finish, 2)


def step(events, labels, counts, gain, w_qkv, w_out, w_piece, table):
    vmem = pl.BlockSpec(memory_space=pltpu.VMEM)
    scratch = [
        pltpu.VMEM((D, 3 * D), BF16),
        pltpu.VMEM((D, D), BF16),
        pltpu.VMEM((D, PIECES * R), BF16),
        pltpu.VMEM((CODES, R), BF16),
        pltpu.SemaphoreType.DMA((4,)),
        pltpu.VMEM((ROWS, EVENTS), BF16),
        pltpu.VMEM((WIN, SLOT, WIDE), BF16),
        pltpu.VMEM((WIN, SLOT, WIDE), BF16),
        pltpu.VMEM((WIN, SLOT, D), BF16),
        pltpu.VMEM((WIN, SLOT, D), BF16),
        pltpu.SemaphoreType.DMA((WIN,)),
        pltpu.SemaphoreType.DMA((WIN,)),
        pltpu.SemaphoreType.DMA((WIN,)),
        pltpu.SemaphoreType.DMA((WIN,)),
        pltpu.SemaphoreType.DMA((N_ITEMS, 10)),
        pltpu.SemaphoreType.DMA((N_ITEMS, 10)),
        pltpu.SemaphoreType.DMA((4, 4)),
        pltpu.SemaphoreType.DMA((4, 4)),
        pltpu.VMEM((WIN, 128, 128), BF16),
        pltpu.VMEM((WIN, 48, 512), BF16),
        pltpu.VMEM((WIN, 48, 384), BF16),
        pltpu.VMEM((3, WIN, 48, 256), BF16),
        pltpu.VMEM((3, WIN, 48, 128), BF16),
        pltpu.VMEM((WIN, SLOT, 128), BF16),
        pltpu.VMEM((D, D), BF16),
        pltpu.VMEM((D, ROWS), BF16),
        pltpu.VMEM((2, 32, 512), F32),
        pltpu.VMEM((ROWS, D), BF16),
        pltpu.VMEM((D, ROWS), BF16),
        pltpu.VMEM((18, ROWS, 128), BF16),
        pltpu.VMEM((PAIRS, 2, ROWS, ROWS), BF16),
        pltpu.VMEM((ROWS, D), BF16),
        pltpu.VMEM((ROWS, D), BF16),
        pltpu.VMEM((PIECES, ROWS, R), BF16),
        pltpu.VMEM((PIECES, R, ROWS), BF16),
        pltpu.VMEM((PIECES, ROWS, R), F32),
        pltpu.VMEM((ROWS, R), F32),
        pltpu.VMEM((PIECES, ROWS, 128), F32),
        pltpu.VMEM((ROWS, PIECES * R), BF16),
        pltpu.VMEM((ROWS, D), BF16),
        pltpu.VMEM((ROWS, D), BF16),
        pltpu.VMEM((ROWS, 3 * D), BF16),
        pltpu.VMEM((ROWS, ROWS), F32),
        pltpu.VMEM((3, ROWS, 128), F32),
        pltpu.VMEM((ROWS, D), F32),
    ]
    for name, rows, width, order in ITEMS:
        last = 32 if name == "t" else 16
        scratch += [
            pltpu.VMEM((4, 4, rows, width), BF16),
            pltpu.VMEM((3, 4, rows, width), BF16),
            pltpu.VMEM((4, rows, width), BF16),
            pltpu.VMEM((3, rows, width), BF16),
            pltpu.VMEM((4, last, width), BF16),
            pltpu.VMEM((3, last, width), BF16),
        ]
    return pl.pallas_call(
        step_kernel,
        out_shape=(
            jax.ShapeDtypeStruct((EVENTS, D), BF16),
            jax.ShapeDtypeStruct((8, 128), F32),
            jax.ShapeDtypeStruct((6, 3 * D), F32),
            jax.ShapeDtypeStruct((6, D), F32),
            jax.ShapeDtypeStruct((6, PIECES * R), F32),
            jax.ShapeDtypeStruct((32, R), F32),
        ),
        in_specs=[vmem] * 4 + [pl.BlockSpec(memory_space=pl.ANY)] * 4,
        out_specs=(vmem,) * 6,
        scratch_shapes=scratch,
        compiler_params=pltpu.CompilerParams(
            collective_id=1, has_side_effects=True, vmem_limit_bytes=63 * 1024 * 1024
        ),
        name="step",
    )(events, labels, counts, gain, w_qkv, w_out, w_piece, table)


def result_kernel(*refs):
    for src, dst in zip(refs[:5], refs[6:11]):
        dst[...] = src[...]
    refs[11][...] = refs[5][0, :6]


def results(rows, g_qkv, g_out, g_piece, g_table, gain):
    vmem = pl.BlockSpec(memory_space=pltpu.VMEM)
    like = [jax.ShapeDtypeStruct(a.shape, a.dtype) for a in (rows, g_qkv, g_out, g_piece, g_table)]
    return pl.pallas_call(
        result_kernel,
        out_shape=(*like, jax.ShapeDtypeStruct((6,), F32)),
        in_specs=[vmem] * 6,
        out_specs=(vmem,) * 6,
        name="results",
    )(rows, g_qkv, g_out, g_piece, g_table, gain)


def body(
    events,
    send_counts,
    patient_ids,
    codes,
    event_piece,
    censor_piece,
    norm_gain,
    w_qkv,
    w_out,
    w_piece,
    code_table,
):
    labels = jnp.concatenate([patient_ids[0], codes[0], event_piece[0], censor_piece[0]], 0)
    rows, gain, g_qkv, g_out, g_piece, g_table = step(
        events[0, 0], labels, send_counts[0], norm_gain[None], w_qkv, w_out, w_piece, code_table
    )
    rows, g_qkv, g_out, g_piece, g_table, g_gain = results(rows, g_qkv, g_out, g_piece, g_table, gain)
    return (rows[None, None], g_gain, g_qkv, g_out, g_piece, g_table)


def solution(mesh):
    split = P("win", "rep")
    return jax.shard_map(
        body,
        mesh=mesh,
        in_specs=(split,) * 6 + (P(),) * 5,
        out_specs=(split,) + (P(("win", "rep")),) * 5,
        check_vma=False,
    )
```
